32 devices in a mesh: grp: 1, dom: 32 (over z, y, x, core).
Axes of the slice: x: 2, y: 2, z: 4, core: 2. Of those that a mesh axis runs over, the one named last changes fastest.
Arguments:
- owned_blips: bfloat16 [128, 32768], P(('grp', 'dom')), may hold values from -6 to 6
- potential: float32 [32, 32, 1024], P('dom', 'grp'), may hold values from -5 to 5
- slot_owner: int32 [768, 1], P(('grp', 'dom')), may hold values from 0 to 31; in each aligned block of 24 rows (0 to 23, 24 to 47, ...) at most 2 rows name the same one
- slot_row: int32 [768], P(('grp', 'dom')), may hold values from 0 to 3
- slot_offset: int32 [768], P(('grp', 'dom')), may hold values from 0 to 31
Outputs:
- blip_gradient: float32 [128, 32768], P(('grp', 'dom'))
- hamiltonian: float32 [128, 128], P(('grp', 'dom'))
The draws below stay inside these ranges and needn't reach their ends.
Inputs may be any that keep to these rules, and one draw needn't show every extreme that they name: `slot_owner`: among the 24 pieces of one device at most 2 name the same owner.
All inputs are finite; a program needn't handle non-finite values.
Results may differ from the reference program's by a relative error of at most 0.012.
The reference program's roundings to bfloat16 on the way (of `slot_blips`, `back_plane` and `gradient_piece`) count: a program that leaves them out, or rounds other values in their place, can miss the bound.
Values may be sent and summed in bfloat16 or wider, within the bound.
A program may use at most 128 MiB of HBM per device.

```python
import math
import jax
import jax.numpy as jnp
import numpy as np
from jax import lax

NB = 32
S_DEV = 4
SLOTS = 24
PY = 32
NN = 1024
NB3 = 32768
CAP = 2
SUPPORTS = 128
N_GRP = 1
N_DOM = 32


def set_ends(entries, stream_key, low, high):
    spot = [jax.random.randint(jax.random.fold_in(stream_key, axis), (), 0, length) for axis, length in enumerate(entries.shape)]
    widest = entries.shape.index(max(entries.shape))
    next_to = spot[:widest] + [(spot[widest] + 1) % entries.shape[widest]] + spot[widest + 1:]
    return entries.at[tuple(spot)].set(low).at[tuple(next_to)].set(high)


def levels(rng, extent, split, smallest, high):
    loudness = 1.0
    for position, parts in split:
        heights = jax.random.uniform(jax.random.fold_in(jax.random.fold_in(rng, 6), position), (parts,), jnp.float32, smallest / len(split), high / len(split))
        loudness = loudness * jnp.repeat(jnp.exp(heights), extent[position] // parts).reshape((-1,) + (1,) * (len(extent) - 1 - position))
    return loudness


def deal_out(key, own, number, rows, number_of, top, most, lean):
    ranking = jax.random.permutation(key, number_of)
    heavy_load, usual = portions_of(number_of, rows * top, most, lean, True), portions_of(number_of, rows * top, most, lean, False)
    places = jnp.arange(number_of)

    def named(tallies, offset_by):
        used = int((tallies > 0).sum())
        fixed = max(1, used // 4)
        moved = fixed + (places - fixed + offset_by * (used - fixed)) % max(1, number_of - fixed)
        return jnp.zeros((number_of,), jnp.int32).at[ranking[jnp.where(places < fixed, places, moved)]].set(jnp.asarray(tallies, jnp.int32))

    tallies = jnp.where(number % 4 == 0, named(heavy_load, number // 4), named(usual, number - number // 4 - 1))
    mixed = jax.random.permutation(jax.random.fold_in(own, 3), number_of)
    giver, taker = mixed[0:number_of // 2 * 2:2], mixed[1:number_of // 2 * 2:2]
    room = jnp.minimum(tallies[giver] - 1, most - tallies[taker]) // 2
    room = jnp.where((giver == ranking[0]) | (taker == ranking[0]) | (tallies[taker] == 0), 0, jnp.maximum(room, 0))
    moved = jax.random.randint(jax.random.fold_in(own, 4), (number_of // 2,), 0, 1 << 20) % (room + 1)
    tallies = tallies.at[giver].add(-moved).at[taker].add(moved)
    members = jnp.searchsorted(jnp.cumsum(tallies), jnp.arange(rows * top), side="right").astype(jnp.int32)
    grid = members.reshape(top, rows).T
    grid = grid[jax.random.permutation(jax.random.fold_in(own, 1), rows)]
    offset_by = jax.random.randint(jax.random.fold_in(own, 2), (rows, 1), 0, top)
    return jnp.take_along_axis(grid, (jnp.arange(top)[None, :] + offset_by) % top, axis=1)


def portions_of(amount, total, bound, lean, full):
    portions = [(1 << 20) // math.isqrt(grade ** lean) + 1 for grade in range(1, amount + 1)]
    largest = bound if full else min(bound, max(-(-total // amount), total * portions[0] // sum(portions)))
    least = 1 if total - largest >= amount - 1 else 0
    counts, surplus = [largest] + [least] * (amount - 1), total - largest - least * (amount - 1)
    while surplus > 0:
        candidates = [i for i in range(1, amount) if counts[i] < largest] or [i for i in range(1, amount) if counts[i] < bound]
        pool, budget = sum([portions[i] for i in candidates]), surplus
        for i in candidates:
            more = min(bound - counts[i], max(1, budget * portions[i] // pool), surplus)
            counts[i] = counts[i] + more
            surplus = surplus - more
    return np.array(counts)


def bell_draw(own_key, dims, scale, bound, cuts=(), kind=jnp.bfloat16):
    gain = levels(own_key, dims, cuts, -0.22, 0.18) if cuts else 1.0
    drawn = jax.random.normal(own_key, dims, jnp.float32) * scale * gain
    return jnp.minimum(jnp.maximum(drawn, -bound), bound).astype(kind)


def setup_inputs(seed: int = 0) -> dict:
    seeds = jax.random.split(jax.random.key(seed), 6)
    owned_blips = bell_draw(seeds[0], (SUPPORTS, NB3), 1.0, 6.0, ((0, 32),))
    potential = bell_draw(seeds[1], (N_DOM, N_GRP * PY, NN), 1.0, 5.0, ((0, 32),), jnp.float32)
    slot_owner_keys = jax.random.split(jax.random.fold_in(seeds[2], 1), (N_GRP * N_DOM * SLOTS) // SLOTS)
    slot_owner_turns = jax.random.permutation(jax.random.fold_in(seeds[2], 3), (N_GRP * N_DOM * SLOTS) // SLOTS)
    slot_owner = jax.vmap(lambda own, number: deal_out(jax.random.fold_in(seeds[2], 2), own, number, SLOTS, N_DOM, 1, CAP, 2))(slot_owner_keys, slot_owner_turns).reshape((N_GRP * N_DOM * SLOTS, 1))
    slot_row = set_ends(jax.random.randint(seeds[3], (N_GRP * N_DOM * SLOTS,), 0, S_DEV), jax.random.fold_in(seeds[3], 1), 0, S_DEV - 1).astype(jnp.int32)
    slot_offset = set_ends(jax.random.randint(seeds[4], (N_GRP * N_DOM * SLOTS,), 0, PY), jax.random.fold_in(seeds[4], 1), 0, PY - 1).astype(jnp.int32)
    return dict(owned_blips=owned_blips, potential=potential, slot_owner=slot_owner, slot_row=slot_row, slot_offset=slot_offset)


def spline_tables():
    cells_line = jnp.arange(NB, dtype=jnp.int32)
    offset = cells_line[:, None] - cells_line[None, :]
    spline = jnp.where(offset == 0, 2.0 / 3.0, jnp.where(jnp.abs(offset) == 1, 1.0 / 6.0, 0.0)).astype(jnp.float32)
    second = jnp.where(offset == 0, -2.0, jnp.where(jnp.abs(offset) == 1, 1.0, 0.0)).astype(jnp.float32)
    plane_value = jnp.einsum("ac,bd->abcd", spline, spline).reshape(NB * NB, NB * NB)
    plane_curve = (jnp.einsum("ac,bd->abcd", second, spline) + jnp.einsum("ac,bd->abcd", spline, second)).reshape(NB * NB, NB * NB)
    return (spline.astype(jnp.bfloat16), second.astype(jnp.bfloat16), plane_value.astype(jnp.bfloat16), plane_curve.astype(jnp.bfloat16))


def domain_terms(slot_blips, window, tables):
    spline, second, plane_value, plane_curve = [table.astype(jnp.float32) for table in tables]
    highest = lax.Precision.HIGHEST
    count_slots = slot_blips.shape[0]
    layered = slot_blips.reshape(count_slots, NB, NB * NB).astype(jnp.float32)
    y_value = jnp.einsum("ya,sab->syb", spline, layered, precision=highest).astype(jnp.bfloat16).astype(jnp.float32)
    y_curve = jnp.einsum("ya,sab->syb", second, layered, precision=highest).astype(jnp.bfloat16).astype(jnp.float32)
    values_grid = jnp.einsum("syb,bc->syc", y_value, plane_value, precision=highest)
    laplace = jnp.einsum("syb,bc->syc", y_curve, plane_value, precision=highest) + jnp.einsum("syb,bc->syc", y_value, plane_curve, precision=highest)
    applied = (-0.5 * laplace + window * values_grid).astype(jnp.bfloat16).astype(jnp.float32)
    values_low = values_grid.astype(jnp.bfloat16).astype(jnp.float32)
    back_plane = jnp.einsum("syb,bc->syc", applied, plane_value, precision=highest).astype(jnp.bfloat16).astype(jnp.float32)
    gradient_piece = jnp.einsum("ay,sab->syb", spline, back_plane, precision=highest).astype(jnp.bfloat16)
    intersection = jnp.einsum("sk,tk->st", values_low.reshape(count_slots, -1), applied.reshape(count_slots, -1), precision=highest) / float(NB * NB * NB)
    return gradient_piece.reshape(count_slots, NB * NB * NB), intersection


def reference(owned_blips, potential, slot_owner, slot_row, slot_offset):
    tables = spline_tables()
    group_blips = owned_blips.reshape(N_GRP, N_DOM * S_DEV, NB * NB * NB)
    owners = slot_owner.reshape(N_GRP, N_DOM, SLOTS).astype(jnp.int32)
    targets = owners * S_DEV + slot_row.reshape(N_GRP, N_DOM, SLOTS).astype(jnp.int32)
    offsets = slot_offset.reshape(N_GRP, N_DOM, SLOTS).astype(jnp.int32)
    columns = jnp.arange(N_DOM * S_DEV, dtype=jnp.int32)

    def one_domain(state_pair, domain_index):
        gradient, hamilton = state_pair
        group_index = (domain_index // N_DOM).astype(jnp.int32)
        domain = (domain_index % N_DOM).astype(jnp.int32)
        target = targets[group_index, domain]
        slot_blips = group_blips[group_index][target]
        field = potential[domain]
        lower_cells = lax.dynamic_slice_in_dim(field, (group_index * PY).astype(jnp.int32), PY, 0)
        upper_cells = lax.dynamic_slice_in_dim(field, (((group_index + 1) % N_GRP) * PY).astype(jnp.int32), PY, 0)
        extended = jnp.concatenate([lower_cells, upper_cells], axis=0)

        def cut_window(first_row):
            return lax.dynamic_slice_in_dim(extended, first_row, NB, 0)

        window = jax.vmap(cut_window)(offsets[group_index, domain])
        gradient_piece, intersection = domain_terms(slot_blips, window, tables)
        gradient = gradient.at[group_index, target].add(gradient_piece.astype(jnp.float32))
        select = (target[:, None] == columns[None, :]).astype(jnp.float32)
        weighted = jnp.dot(intersection, select, precision=lax.Precision.HIGHEST)
        hamilton = hamilton.at[group_index].add(jnp.dot(select.T, weighted, precision=lax.Precision.HIGHEST))
        return (gradient, hamilton), None

    start_state = (jnp.zeros((N_GRP, N_DOM * S_DEV, NB * NB * NB), jnp.float32), jnp.zeros((N_GRP, N_DOM * S_DEV, N_DOM * S_DEV), jnp.float32))
    final_state, unused = lax.scan(one_domain, start_state, jnp.arange(N_GRP * N_DOM, dtype=jnp.int32))
    gradient, hamilton = final_state
    return (gradient.reshape(N_GRP * N_DOM * S_DEV, NB * NB * NB), hamilton.reshape(N_GRP * N_DOM * S_DEV, N_DOM * S_DEV))
```

```python
import functools

import jax
import jax.numpy as jnp
import numpy as np
from jax import lax
from jax.experimental import pallas as pl
from jax.experimental.pallas import tpu as pltpu
from jax.sharding import PartitionSpec as P

NB = 32
HALF = NB // 2
PLANE = NB * NB
VMEM_LIMIT = 56 * 2**20
MESH = pl.DeviceIdType.MESH
HIGHEST = lax.Precision.HIGHEST


def spline_tables():
    cells_line = np.arange(NB, dtype=np.int32)
    offset = cells_line[:, None] - cells_line[None, :]
    spline = np.where(
        offset == 0, 2.0 / 3.0, np.where(np.abs(offset) == 1, 1.0 / 6.0, 0.0)
    ).astype(np.float32)
    second = np.where(offset == 0, -2.0, np.where(np.abs(offset) == 1, 1.0, 0.0)).astype(np.float32)
    plane_value = np.einsum("ac,bd->abcd", spline, spline).reshape(PLANE, PLANE)
    plane_curve = (
        np.einsum("ac,bd->abcd", second, spline) + np.einsum("ac,bd->abcd", spline, second)
    ).reshape(PLANE, PLANE)
    low = jnp.bfloat16
    return spline.astype(low), second.astype(low), plane_value.astype(low), plane_curve.astype(low)


def passed_along(block, axis, distance):
    devices = range(lax.axis_size(axis))
    route = [((i - distance) % len(devices), i) for i in devices]
    return lax.ppermute(block, axis, route)


def digits(index, depth):
    core = index % 2
    a = (index // 2) % 2
    b = (index // 4) % 2
    z = index // 8
    return z, b, a, core


def place(index, depth, order):
    z, b, a, core = digits(index, depth)
    first, second = (a, b) if order == 0 else (b, a)
    return ((core * 2 + first) * 2 + second) * depth + z


def position(depth):
    me = lax.axis_index("dom")
    z, b, a, core = digits(me, depth)
    to_core = me + 1 - 2 * core
    to_a = me + 2 * (1 - 2 * a)
    to_b = me + 4 * (1 - 2 * b)
    along = [lax.rem(z + dz, depth) for dz in range(1, depth)]
    to_z = [me + 8 * (other - z) for other in along]
    return (z, b, a, core), to_core, to_a, to_b, along, to_z


def meet(partners):
    barrier = pltpu.get_barrier_semaphore()
    for partner in partners:
        pl.semaphore_signal(barrier, inc=1, device_id={"dom": partner}, device_id_type=MESH)
    pl.semaphore_wait(barrier, len(partners))


def gather_kernel(depth, rows, own_ref, got_a, got_b, send, recv, local):
    (z, b, a, core), to_core, to_a, to_b, along, to_z = position(depth)
    meet([to_core, to_a, to_b] + to_z)
    got = (got_a, got_b)
    firsts, seconds = (a, b), (b, a)
    to_first, to_second = (to_a, to_b), (to_b, to_a)

    def remote(src, dst, order, row, phase, target):
        return pltpu.make_async_remote_copy(
            src_ref=src,
            dst_ref=dst,
            send_sem=send.at[order, row, phase],
            recv_sem=recv.at[order, row, phase],
            device_id={"dom": target},
            device_id_type=MESH,
        )

    def base(order):
        return ((core * 2 + firsts[order]) * 2 + seconds[order]) * depth

    own, wide = {}, {}
    for row in range(rows):
        for order in range(2):
            piece = own_ref.at[row, pl.ds(order * HALF, HALF)]
            spot = got[order].at[row, base(order) + z]
            for dz in range(1, depth):
                copy = remote(piece, spot, order, row, dz - 1, to_z[dz - 1])
                copy.start()
                wide[order, row, dz - 1] = copy
            copy = pltpu.make_async_copy(piece, spot, local.at[order, row])
            copy.start()
            own[order, row] = copy

    def go(order, row, phase):
        if phase == 0:
            own[order, row].wait()
            for dz in range(1, depth):
                wide[order, row, dz - 1].wait_recv()
            start, size, target = base(order), depth, to_second[order]
        else:
            wide[order, row, depth - 2 + phase].wait_recv()
            if phase == 1:
                start = (core * 2 + firsts[order]) * 2 * depth
                size, target = 2 * depth, to_first[order]
            else:
                start, size, target = core * 4 * depth, 4 * depth, to_core
        block = got[order].at[row, pl.ds(start, size)]
        copy = remote(block, block, order, row, depth - 1 + phase, target)
        copy.start()
        wide[order, row, depth - 1 + phase] = copy

    for step in range(rows + 2):
        for phase in range(3):
            row = step - phase
            if 0 <= row < rows:
                for order in range(2):
                    go(order, row, phase)
    for row in range(rows):
        for order in range(2):
            wide[order, row, depth + 1].wait_recv()
            for phase in range(depth + 2):
                wide[order, row, phase].wait_send()


def gather(own, depth):
    rows = own.shape[0]
    half = jax.ShapeDtypeStruct((rows, 8 * depth, HALF, PLANE), own.dtype)
    return pl.pallas_call(
        functools.partial(gather_kernel, depth, rows),
        out_shape=(half, half),
        in_specs=[pl.BlockSpec(memory_space=pl.ANY)],
        out_specs=[pl.BlockSpec(memory_space=pl.ANY)] * 2,
        scratch_shapes=[
            pltpu.SemaphoreType.DMA((2, rows, depth + 2)),
            pltpu.SemaphoreType.DMA((2, rows, depth + 2)),
            pltpu.SemaphoreType.DMA((2, rows)),
        ],
        compiler_params=pltpu.CompilerParams(collective_id=0, has_side_effects=True),
    )(own)


def domain_kernel(
    group,
    steps,
    place_a,
    place_b,
    row_of,
    offset_of,
    *refs,
):
    blips_a, blips_b = refs[:group], refs[group : 2 * group]
    (field, wide_y, back_y, value_ref, curve_ref, hot_row, hot_column) = refs[2 * group : 2 * group + 7]
    out_a, out_b, out_h, low_ref, applied_ref = refs[2 * group + 7 :]
    step = pl.program_id(0)
    block = group * NB

    @pl.when(step == 0)
    def _():
        zero = jnp.zeros((HALF, PLANE), jnp.bfloat16)
        for row in range(out_a.shape[0]):

            @pl.loop(0, out_a.shape[1])
            def _(spot):
                out_a[row, spot] = zero
                out_b[row, spot] = zero

    blips = jnp.concatenate(
        [half[0, 0] for pair in zip(blips_a, blips_b) for half in pair], axis=0
    )
    both = jnp.dot(wide_y[...], blips, preferred_element_type=jnp.float32).astype(jnp.bfloat16)
    y_value, y_curve = both[:block], both[block:]
    value = value_ref[...]
    values_grid = jnp.dot(y_value, value, preferred_element_type=jnp.float32)
    laplace = jnp.dot(y_curve, value, preferred_element_type=jnp.float32) + jnp.dot(
        y_value, curve_ref[...], preferred_element_type=jnp.float32
    )
    cuts = []
    for k in range(group):
        offset = offset_of[step * group + k]
        near = field[pl.ds(pl.multiple_of(offset // 8 * 8, 8), NB + 8), :]
        cuts.append(pltpu.roll(near, lax.rem(NB + 8 - offset % 8, NB + 8), 0)[:NB])
    window = jnp.concatenate(cuts, axis=0)
    applied = (-0.5 * laplace + window * values_grid).astype(jnp.bfloat16)
    here = pl.ds(pl.multiple_of(step * block, block), block)
    low_ref[here, :] = values_grid.astype(jnp.bfloat16)
    applied_ref[here, :] = applied
    back_plane = jnp.dot(applied, value, preferred_element_type=jnp.float32).astype(jnp.bfloat16)
    piece = jnp.dot(back_y[...], back_plane, preferred_element_type=jnp.float32).astype(
        jnp.bfloat16
    )
    for k in range(group):
        slot = step * group + k
        for out, spot, first in (
            (out_a, place_a[slot], k * NB),
            (out_b, place_b[slot], k * NB + HALF),
        ):
            row = row_of[slot]
            total = out[row, spot].astype(jnp.float32) + piece[first : first + HALF].astype(
                jnp.float32
            )
            out[row, spot] = total.astype(jnp.bfloat16)

    @pl.when(step == steps - 1)
    def _():
        gram = lax.dot_general(
            low_ref[...],
            applied_ref[...],
            (((1,), (1,)), ((), ())),
            preferred_element_type=jnp.float32,
        )
        cell_row = lax.broadcasted_iota(jnp.int32, gram.shape, 0) % NB
        cell_column = lax.broadcasted_iota(jnp.int32, gram.shape, 1) % NB
        terms = jnp.where(cell_row == cell_column, gram, 0.0) / float(NB * PLANE)
        count = gram.shape[0]
        to_column = (
            hot_column[...]
            == lax.broadcasted_iota(jnp.int32, (count, out_h.shape[1]), 1)
        ).astype(jnp.float32)
        to_row = (
            hot_row[...] == lax.broadcasted_iota(jnp.int32, (out_h.shape[0], count), 0)
        ).astype(jnp.float32)
        by_column = jnp.dot(
            terms, to_column, precision=HIGHEST, preferred_element_type=jnp.float32
        )
        out_h[...] = jnp.dot(
            to_row, by_column, precision=HIGHEST, preferred_element_type=jnp.float32
        )


def domain(got_a, got_b, field, owner, row, offset, depth):
    rows, owners = got_a.shape[:2]
    slots = owner.shape[0]
    group = next(g for g in (8, 6, 4, 3, 2, 1) if slots % g == 0)
    steps = slots // group
    spline, second, plane_value, plane_curve = spline_tables()
    eye = np.eye(group, dtype=np.float32)
    spread = lambda table: np.kron(eye, table.astype(np.float32)).astype(jnp.bfloat16)
    wide_y = np.concatenate([spread(spline), spread(second)], axis=0)
    back_y = spread(spline.T)
    place_a, place_b = place(owner, depth, 0), place(owner, depth, 1)
    hot_row = jnp.repeat(place_a * 8 + row, NB)[None, :]
    hot_column = jnp.repeat(owner * rows + row, NB)[:, None]

    def pick(k, which):
        def index(i, at_a, at_b, row_of, offset_of):
            slot = i * group + k
            return (row_of[slot], (at_a if which == 0 else at_b)[slot], 0, 0)

        return pl.BlockSpec((1, 1, HALF, PLANE), index)

    whole = lambda shape: pl.BlockSpec(shape, lambda i, *_: (0,) * len(shape))
    once = lambda shape: pl.BlockSpec(
        shape, lambda i, *_: (0,) * len(shape), pipeline_mode=pl.Buffered(1)
    )
    fixed = (
        field,
        jnp.asarray(wide_y),
        jnp.asarray(back_y),
        jnp.asarray(plane_value),
        jnp.asarray(plane_curve),
        hot_row,
        hot_column,
    )
    dense = jax.ShapeDtypeStruct((rows, owners, HALF, PLANE), jnp.bfloat16)
    flop = 2 * slots * NB * PLANE * PLANE * 4
    return pl.pallas_call(
        functools.partial(domain_kernel, group, steps),
        grid_spec=pltpu.PrefetchScalarGridSpec(
            num_scalar_prefetch=4,
            grid=(steps,),
            in_specs=[pick(k, 0) for k in range(group)]
            + [pick(k, 1) for k in range(group)]
            + [once(x.shape) for x in fixed],
            out_specs=[whole(dense.shape), whole(dense.shape), whole((owners * 8, owners * rows))],
            scratch_shapes=[
                pltpu.VMEM((slots * NB, PLANE), jnp.bfloat16),
                pltpu.VMEM((slots * NB, PLANE), jnp.bfloat16),
            ],
        ),
        out_shape=(
            dense,
            dense,
            jax.ShapeDtypeStruct((owners * 8, owners * rows), jnp.float32),
        ),
        compiler_params=pltpu.CompilerParams(
            vmem_limit_bytes=VMEM_LIMIT, dimension_semantics=("arbitrary",)
        ),
        cost_estimate=pl.CostEstimate(flops=flop, bytes_accessed=2**24, transcendentals=0),
    )(place_a, place_b, row, offset, *([got_a] * group), *([got_b] * group), *fixed)


def scatter_kernel(depth, rows, part_a, part_b, part_h, grad, ham, *scratch):
    (z, b, a, core), to_core, to_a, to_b, along, to_z = position(depth)
    buffers = (scratch[0:4], scratch[4:8], scratch[8:12])
    send, recv = scratch[12:14]
    meet([to_core, to_a, to_b] + to_z)
    parts = (part_a, part_b, part_h)
    firsts, seconds = (a, b, a), (b, a, b)
    to_first, to_second = (to_a, to_b, to_a), (to_b, to_a, to_b)
    flight = {}

    def remote(src, dst, stream, row, phase, target):
        copy = pltpu.make_async_remote_copy(
            src_ref=src,
            dst_ref=dst,
            send_sem=send.at[stream, row, phase],
            recv_sem=recv.at[stream, row, phase],
            device_id={"dom": target},
            device_id_type=MESH,
        )
        copy.start()
        flight[stream, row, phase] = copy

    def add(stream, row, level, source, start, size):
        into = buffers[stream][level]

        @pl.loop(0, size)
        def _(i):
            total = into[row, i].astype(jnp.float32) + source[row, start + i].astype(jnp.float32)
            into[row, i] = total.astype(into.dtype)

    def go(stream, row, phase):
        first, second, zone, last = buffers[stream]
        part = parts[stream]
        if phase == 0:
            remote(
                part.at[row, pl.ds((1 - core) * 4 * depth, 4 * depth)],
                first.at[row], stream, row, 0, to_core,
            )
        elif phase == 1:
            flight[stream, row, 0].wait_recv()
            add(stream, row, 0, part, core * 4 * depth, 4 * depth)
            remote(
                first.at[row, pl.ds((1 - firsts[stream]) * 2 * depth, 2 * depth)],
                second.at[row], stream, row, 1, to_first[stream],
            )
        elif phase == 2:
            flight[stream, row, 1].wait_recv()
            add(stream, row, 1, first, firsts[stream] * 2 * depth, 2 * depth)
            remote(
                second.at[row, pl.ds((1 - seconds[stream]) * depth, depth)],
                zone.at[row], stream, row, 2, to_second[stream],
            )
        elif phase == 3:
            flight[stream, row, 2].wait_recv()
            add(stream, row, 2, second, seconds[stream] * depth, depth)
            for dz in range(1, depth):
                remote(
                    zone.at[row, along[dz - 1]],
                    last.at[row, dz - 1], stream, row, 2 + dz, to_z[dz - 1],
                )
        else:
            for dz in range(1, depth):
                flight[stream, row, 2 + dz].wait_recv()
            total = zone[row, z].astype(jnp.float32)
            for dz in range(1, depth):
                total = total + last[row, dz - 1].astype(jnp.float32)
            if stream == 2:
                ham[...] = total
            else:
                grad[row, stream * HALF : (stream + 1) * HALF, :] = total

    chunks = [[(2, 0), (0, 0), (1, 0)]] + [[(0, row), (1, row)] for row in range(1, rows)]
    for chunk in chunks:
        for stream, row in chunk:
            go(stream, row, 0)
    for step in range(len(chunks) + 3):
        for phase in range(1, 5):
            at = step - (phase - 1)
            if 0 <= at < len(chunks):
                for stream, row in chunks[at]:
                    go(stream, row, phase)
    for copy in flight.values():
        copy.wait_send()


def scatter(part_a, part_b, part_h, depth):
    rows = part_a.shape[0]
    columns = part_h.shape[-1]
    low = lambda count: pltpu.VMEM((rows, count, HALF, PLANE), jnp.bfloat16)
    full = lambda count: pltpu.VMEM((1, count, 8, columns), jnp.float32)
    sizes = (4 * depth, 2 * depth, depth, depth - 1)
    return pl.pallas_call(
        functools.partial(scatter_kernel, depth, rows),
        out_shape=(
            jax.ShapeDtypeStruct((rows, NB, PLANE), jnp.float32),
            jax.ShapeDtypeStruct((8, columns), jnp.float32),
        ),
        in_specs=[pl.BlockSpec(memory_space=pltpu.VMEM)] * 3,
        out_specs=[pl.BlockSpec(memory_space=pltpu.VMEM)] * 2,
        scratch_shapes=[low(n) for n in sizes]
        + [low(n) for n in sizes]
        + [full(n) for n in sizes]
        + [
            pltpu.SemaphoreType.DMA((3, rows, depth + 2)),
            pltpu.SemaphoreType.DMA((3, rows, depth + 2)),
        ],
        compiler_params=pltpu.CompilerParams(
            collective_id=1, has_side_effects=True, vmem_limit_bytes=VMEM_LIMIT
        ),
    )(part_a, part_b, part_h)


def on_device(owned_blips, potential, slot_owner, slot_row, slot_offset):
    devices = lax.axis_size("dom")
    depth = devices // 8
    rows = owned_blips.shape[0]
    owner = slot_owner[:, 0]
    upper = potential if lax.axis_size("grp") == 1 else passed_along(potential, "grp", -1)
    field = jnp.concatenate([potential[0], upper[0]], axis=0)
    got_a, got_b = gather(owned_blips.reshape(rows, NB, PLANE), depth)
    part_a, part_b, part_h = domain(got_a, got_b, field, owner, slot_row, slot_offset, depth)
    grad, ham = scatter(part_a, part_b, part_h.reshape(1, devices, 8, -1), depth)
    return grad.reshape(rows, -1), ham[:rows]


def solution(mesh):
    placed = (
        P(("grp", "dom"), None),
        P("dom", "grp", None),
        P(("grp", "dom"), None),
        P(("grp", "dom")),
        P(("grp", "dom")),
    )
    return jax.shard_map(
        on_device,
        mesh=mesh,
        in_specs=placed,
        out_specs=(P(("grp", "dom"), None), P(("grp", "dom"), None)),
        check_vma=False,
    )
```

```python
import functools

import jax
import jax.numpy as jnp
import numpy as np
from jax import lax
from jax.experimental import pallas as pl
from jax.experimental.pallas import tpu as pltpu
from jax.sharding import PartitionSpec as P

NB = 32
HALF = NB // 2
PLANE = NB * NB
VMEM_LIMIT = 56 * 2**20
MESH = pl.DeviceIdType.MESH
HIGHEST = lax.Precision.HIGHEST


def spline_tables():
    cells_line = np.arange(NB, dtype=np.int32)
    offset = cells_line[:, None] - cells_line[None, :]
    spline = np.where(
        offset == 0, 2.0 / 3.0, np.where(np.abs(offset) == 1, 1.0 / 6.0, 0.0)
    ).astype(np.float32)
    second = np.where(offset == 0, -2.0, np.where(np.abs(offset) == 1, 1.0, 0.0)).astype(np.float32)
    plane_value = np.einsum("ac,bd->abcd", spline, spline).reshape(PLANE, PLANE)
    plane_curve = (
        np.einsum("ac,bd->abcd", second, spline) + np.einsum("ac,bd->abcd", spline, second)
    ).reshape(PLANE, PLANE)
    low = jnp.bfloat16
    return spline.astype(low), second.astype(low), plane_value.astype(low), plane_curve.astype(low)


def passed_along(block, axis, distance):
    devices = range(lax.axis_size(axis))
    route = [((i - distance) % len(devices), i) for i in devices]
    return lax.ppermute(block, axis, route)


def digits(index, depth):
    core = index % 2
    a = (index // 2) % 2
    b = (index // 4) % 2
    z = index // 8
    return z, b, a, core


def place(index, depth, order):
    z, b, a, core = digits(index, depth)
    first, second = (a, b) if order == 0 else (b, a)
    return ((core * 2 + first) * 2 + second) * depth + z


def position(depth):
    me = lax.axis_index("dom")
    z, b, a, core = digits(me, depth)
    to_core = me + 1 - 2 * core
    to_a = me + 2 * (1 - 2 * a)
    to_b = me + 4 * (1 - 2 * b)
    along = [lax.rem(z + dz, depth) for dz in range(1, depth)]
    to_z = [me + 8 * (other - z) for other in along]
    return (z, b, a, core), to_core, to_a, to_b, along, to_z


def meet(partners):
    barrier = pltpu.get_barrier_semaphore()
    for partner in partners:
        pl.semaphore_signal(barrier, inc=1, device_id={"dom": partner}, device_id_type=MESH)
    pl.semaphore_wait(barrier, len(partners))


def gather_kernel(depth, rows, own_ref, got_a, got_b, send, recv, local):
    (z, b, a, core), to_core, to_a, to_b, along, to_z = position(depth)
    meet([to_core, to_a, to_b] + to_z)
    got = (got_a, got_b)
    firsts, seconds = (a, b), (b, a)
    to_first, to_second = (to_a, to_b), (to_b, to_a)

    def remote(src, dst, order, row, phase, target):
        return pltpu.make_async_remote_copy(
            src_ref=src,
            dst_ref=dst,
            send_sem=send.at[order, row, phase],
            recv_sem=recv.at[order, row, phase],
            device_id={"dom": target},
            device_id_type=MESH,
        )

    def base(order):
        return ((core * 2 + firsts[order]) * 2 + seconds[order]) * depth

    own, wide = {}, {}

    def begin(row):
        for order in range(2):
            piece = own_ref.at[row, pl.ds(order * HALF, HALF)]
            spot = got[order].at[row, base(order) + z]
            for dz in range(1, depth):
                copy = remote(piece, spot, order, row, dz - 1, to_z[dz - 1])
                copy.start()
                wide[order, row, dz - 1] = copy
            copy = pltpu.make_async_copy(piece, spot, local.at[order, row])
            copy.start()
            own[order, row] = copy

    def go(order, row, phase):
        if phase == 0:
            if order == 0 and row + 1 < rows:
                begin(row + 1)
            own[order, row].wait()
            for dz in range(1, depth):
                wide[order, row, dz - 1].wait_recv()
            start, size, target = base(order), depth, to_second[order]
        else:
            wide[order, row, depth - 2 + phase].wait_recv()
            if phase == 1:
                start = (core * 2 + firsts[order]) * 2 * depth
                size, target = 2 * depth, to_first[order]
            else:
                start, size, target = core * 4 * depth, 4 * depth, to_core
        block = got[order].at[row, pl.ds(start, size)]
        copy = remote(block, block, order, row, depth - 1 + phase, target)
        copy.start()
        wide[order, row, depth - 1 + phase] = copy

    begin(0)
    for step in range(rows + 2):
        for phase in range(3):
            row = step - phase
            if 0 <= row < rows:
                for order in range(2):
                    go(order, row, phase)
    for row in range(rows):
        for order in range(2):
            wide[order, row, depth + 1].wait_recv()
            for phase in range(depth + 2):
                wide[order, row, phase].wait_send()


def gather(own, depth):
    rows = own.shape[0]
    half = jax.ShapeDtypeStruct((rows, 8 * depth, HALF, PLANE), own.dtype)
    return pl.pallas_call(
        functools.partial(gather_kernel, depth, rows),
        out_shape=(half, half),
        in_specs=[pl.BlockSpec(memory_space=pl.ANY)],
        out_specs=[pl.BlockSpec(memory_space=pl.ANY)] * 2,
        scratch_shapes=[
            pltpu.SemaphoreType.DMA((2, rows, depth + 2)),
            pltpu.SemaphoreType.DMA((2, rows, depth + 2)),
            pltpu.SemaphoreType.DMA((2, rows)),
        ],
        compiler_params=pltpu.CompilerParams(collective_id=0, has_side_effects=True),
    )(own)


def domain_kernel(
    group,
    steps,
    depth,
    owner_of,
    row_of,
    offset_of,
    *refs,
):
    blips_a, blips_b = refs[:group], refs[group : 2 * group]
    (lower, upper, wide_y, back_y, value_ref, curve_ref) = refs[2 * group : 2 * group + 6]
    out_a, out_b, out_h, low_ref, applied_ref, field = refs[2 * group + 6 :]
    step = pl.program_id(0)
    block = group * NB

    @pl.when(step == 0)
    def _():
        count = lower.shape[0]
        field[:count] = lower[...]
        field[count:] = upper[...]
        zero = jnp.zeros((HALF, PLANE), jnp.bfloat16)
        for row in range(out_a.shape[0]):

            @pl.loop(0, out_a.shape[1])
            def _(spot):
                out_a[row, spot] = zero
                out_b[row, spot] = zero

    blips = jnp.concatenate(
        [half[0, 0] for pair in zip(blips_a, blips_b) for half in pair], axis=0
    )
    both = jnp.dot(wide_y[...], blips, preferred_element_type=jnp.float32).astype(jnp.bfloat16)
    y_value, y_curve = both[:block], both[block:]
    value = value_ref[...]
    values_grid = jnp.dot(y_value, value, preferred_element_type=jnp.float32)
    laplace = jnp.dot(y_curve, value, preferred_element_type=jnp.float32) + jnp.dot(
        y_value, curve_ref[...], preferred_element_type=jnp.float32
    )
    cuts = []
    for k in range(group):
        offset = offset_of[step * group + k]
        near = field[pl.ds(pl.multiple_of(offset // 8 * 8, 8), NB + 8), :]
        cuts.append(pltpu.roll(near, lax.rem(NB + 8 - offset % 8, NB + 8), 0)[:NB])
    window = jnp.concatenate(cuts, axis=0)
    applied = (-0.5 * laplace + window * values_grid).astype(jnp.bfloat16)
    here = pl.ds(pl.multiple_of(step * block, block), block)
    low_ref[here, :] = values_grid.astype(jnp.bfloat16)
    applied_ref[here, :] = applied
    back_plane = jnp.dot(applied, value, preferred_element_type=jnp.float32).astype(jnp.bfloat16)
    piece = jnp.dot(back_y[...], back_plane, preferred_element_type=jnp.float32).astype(
        jnp.bfloat16
    )
    for k in range(group):
        slot = step * group + k
        for out, order, first in ((out_a, 0, k * NB), (out_b, 1, k * NB + HALF)):
            spot = place(owner_of[slot, 0], depth, order)
            row = row_of[slot]
            total = out[row, spot].astype(jnp.float32) + piece[first : first + HALF].astype(
                jnp.float32
            )
            out[row, spot] = total.astype(jnp.bfloat16)

    @pl.when(step == steps - 1)
    def _():
        gram = lax.dot_general(
            low_ref[...],
            applied_ref[...],
            (((1,), (1,)), ((), ())),
            preferred_element_type=jnp.float32,
        )
        cell_row = lax.broadcasted_iota(jnp.int32, gram.shape, 0) % NB
        cell_column = lax.broadcasted_iota(jnp.int32, gram.shape, 1) % NB
        terms = jnp.where(cell_row == cell_column, gram, 0.0) / float(NB * PLANE)
        count = gram.shape[0]
        slot = lax.broadcasted_iota(jnp.int32, (1, count), 1) // NB
        hot_row, hot_column = jnp.zeros_like(slot), jnp.zeros_like(slot)
        for k in range(count // NB):
            owner, row = owner_of[k, 0], row_of[k]
            hot_row = jnp.where(slot == k, place(owner, depth, 0) * 8 + row, hot_row)
            hot_column = jnp.where(slot == k, owner * out_a.shape[0] + row, hot_column)
        to_column = (
            hot_column == lax.broadcasted_iota(jnp.int32, (out_h.shape[1], count), 0)
        ).astype(jnp.float32)
        to_row = (
            hot_row == lax.broadcasted_iota(jnp.int32, (out_h.shape[0], count), 0)
        ).astype(jnp.float32)
        by_column = lax.dot_general(
            terms,
            to_column,
            (((1,), (1,)), ((), ())),
            precision=HIGHEST,
            preferred_element_type=jnp.float32,
        )
        out_h[...] = jnp.dot(
            to_row, by_column, precision=HIGHEST, preferred_element_type=jnp.float32
        )


def domain(got_a, got_b, lower, upper, owner, row, offset, depth):
    rows, owners = got_a.shape[:2]
    slots = owner.shape[0]
    group = next(g for g in (8, 6, 4, 3, 2, 1) if slots % g == 0)
    steps = slots // group
    spline, second, plane_value, plane_curve = spline_tables()
    eye = np.eye(group, dtype=np.float32)
    spread = lambda table: np.kron(eye, table.astype(np.float32)).astype(jnp.bfloat16)
    wide_y = np.concatenate([spread(spline), spread(second)], axis=0)
    back_y = spread(spline.T)

    def pick(k, which):
        def index(i, owner_of, row_of, offset_of):
            slot = i * group + k
            return (row_of[slot], place(owner_of[slot, 0], depth, which), 0, 0)

        return pl.BlockSpec((1, 1, HALF, PLANE), index)

    whole = lambda shape: pl.BlockSpec(shape, lambda i, *_: (0,) * len(shape))
    once = lambda shape: pl.BlockSpec(
        shape, lambda i, *_: (0,) * len(shape), pipeline_mode=pl.Buffered(1)
    )
    fixed = (
        lower,
        upper,
        jnp.asarray(wide_y),
        jnp.asarray(back_y),
        jnp.asarray(plane_value),
        jnp.asarray(plane_curve),
    )
    dense = jax.ShapeDtypeStruct((rows, owners, HALF, PLANE), jnp.bfloat16)
    flop = 2 * slots * NB * PLANE * PLANE * 4
    return pl.pallas_call(
        functools.partial(domain_kernel, group, steps, depth),
        grid_spec=pltpu.PrefetchScalarGridSpec(
            num_scalar_prefetch=3,
            grid=(steps,),
            in_specs=[pick(k, 0) for k in range(group)]
            + [pick(k, 1) for k in range(group)]
            + [once(x.shape) for x in fixed],
            out_specs=[whole(dense.shape), whole(dense.shape), whole((owners * 8, owners * rows))],
            scratch_shapes=[
                pltpu.VMEM((slots * NB, PLANE), jnp.bfloat16),
                pltpu.VMEM((slots * NB, PLANE), jnp.bfloat16),
                pltpu.VMEM((2 * lower.shape[0], PLANE), jnp.float32),
            ],
        ),
        out_shape=(
            dense,
            dense,
            jax.ShapeDtypeStruct((owners * 8, owners * rows), jnp.float32),
        ),
        compiler_params=pltpu.CompilerParams(
            vmem_limit_bytes=VMEM_LIMIT, dimension_semantics=("arbitrary",)
        ),
        cost_estimate=pl.CostEstimate(flops=flop, bytes_accessed=2**24, transcendentals=0),
    )(owner, row, offset, *([got_a] * group), *([got_b] * group), *fixed)


def scatter_kernel(depth, rows, part_a, part_b, part_h, grad, ham, *scratch):
    (z, b, a, core), to_core, to_a, to_b, along, to_z = position(depth)
    buffers = (scratch[0:4], scratch[4:8], scratch[8:12])
    send, recv, local = scratch[12:15]
    mine = scratch[15:17]
    held = {}
    for row in range(rows):
        for stream, part in enumerate((part_a, part_b)):
            copy = pltpu.make_async_copy(
                part.at[row, pl.ds(core * 4 * depth, 4 * depth)],
                mine[stream].at[row],
                local.at[stream, row],
            )
            copy.start()
            held[stream, row] = copy
    meet([to_core, to_a, to_b] + to_z)
    parts = (part_a, part_b, part_h)
    firsts, seconds = (a, b, a), (b, a, b)
    to_first, to_second = (to_a, to_b, to_a), (to_b, to_a, to_b)
    flight = {}

    def remote(src, dst, stream, row, phase, target):
        copy = pltpu.make_async_remote_copy(
            src_ref=src,
            dst_ref=dst,
            send_sem=send.at[stream, row, phase],
            recv_sem=recv.at[stream, row, phase],
            device_id={"dom": target},
            device_id_type=MESH,
        )
        copy.start()
        flight[stream, row, phase] = copy

    def add(stream, row, level, source, start, size):
        into = buffers[stream][level]

        @pl.loop(0, size, unroll=2)
        def _(i):
            into[row, i] = into[row, i] + source[row, start + i]

    def go(stream, row, phase):
        first, second, zone, last = buffers[stream]
        part = parts[stream]
        if phase == 0:
            remote(
                part.at[row, pl.ds((1 - core) * 4 * depth, 4 * depth)],
                first.at[row], stream, row, 0, to_core,
            )
        elif phase == 1:
            flight[stream, row, 0].wait_recv()
            if stream == 2:
                add(stream, row, 0, part, core * 4 * depth, 4 * depth)
            else:
                held[stream, row].wait()
                add(stream, row, 0, mine[stream], 0, 4 * depth)
            remote(
                first.at[row, pl.ds((1 - firsts[stream]) * 2 * depth, 2 * depth)],
                second.at[row], stream, row, 1, to_first[stream],
            )
        elif phase == 2:
            flight[stream, row, 1].wait_recv()
            add(stream, row, 1, first, firsts[stream] * 2 * depth, 2 * depth)
            remote(
                second.at[row, pl.ds((1 - seconds[stream]) * depth, depth)],
                zone.at[row], stream, row, 2, to_second[stream],
            )
        elif phase == 3:
            flight[stream, row, 2].wait_recv()
            add(stream, row, 2, second, seconds[stream] * depth, depth)
            for dz in range(1, depth):
                remote(
                    zone.at[row, along[dz - 1]],
                    last.at[row, dz - 1], stream, row, 2 + dz, to_z[dz - 1],
                )
        else:
            for dz in range(1, depth):
                flight[stream, row, 2 + dz].wait_recv()
            total = zone[row, z].astype(jnp.float32)
            for dz in range(1, depth):
                total = total + last[row, dz - 1].astype(jnp.float32)
            if stream == 2:
                ham[...] = total
            else:
                grad[row, stream * HALF : (stream + 1) * HALF, :] = total

    chunks = [[(2, 0), (0, 0), (1, 0)]] + [[(0, row), (1, row)] for row in range(1, rows)]
    for chunk in chunks:
        for stream, row in chunk:
            go(stream, row, 0)
    for step in range(len(chunks) + 3):
        for phase in range(1, 5):
            at = step - (phase - 1)
            if 0 <= at < len(chunks):
                for stream, row in chunks[at]:
                    go(stream, row, phase)
    for copy in flight.values():
        copy.wait_send()


def scatter(part_a, part_b, part_h, depth):
    rows = part_a.shape[0]
    columns = part_h.shape[-1]
    low = lambda count: pltpu.VMEM((rows, count, HALF, PLANE), jnp.bfloat16)
    full = lambda count: pltpu.VMEM((1, count, 8, columns), jnp.float32)
    sizes = (4 * depth, 2 * depth, depth, depth - 1)
    return pl.pallas_call(
        functools.partial(scatter_kernel, depth, rows),
        out_shape=(
            jax.ShapeDtypeStruct((rows, NB, PLANE), jnp.float32),
            jax.ShapeDtypeStruct((8, columns), jnp.float32),
        ),
        in_specs=[pl.BlockSpec(memory_space=pl.ANY)] * 2
        + [pl.BlockSpec(memory_space=pltpu.VMEM)],
        out_specs=[pl.BlockSpec(memory_space=pltpu.VMEM)] * 2,
        scratch_shapes=[low(n) for n in sizes]
        + [low(n) for n in sizes]
        + [full(n) for n in sizes]
        + [
            pltpu.SemaphoreType.DMA((3, rows, depth + 2)),
            pltpu.SemaphoreType.DMA((3, rows, depth + 2)),
            pltpu.SemaphoreType.DMA((2, rows)),
        ]
        + [low(sizes[0])] * 2,
        compiler_params=pltpu.CompilerParams(
            collective_id=1, has_side_effects=True, vmem_limit_bytes=VMEM_LIMIT
        ),
    )(part_a, part_b, part_h)


def on_device(owned_blips, potential, slot_owner, slot_row, slot_offset):
    devices = lax.axis_size("dom")
    depth = devices // 8
    rows = owned_blips.shape[0]
    upper = potential if lax.axis_size("grp") == 1 else passed_along(potential, "grp", -1)
    got_a, got_b = gather(owned_blips.reshape(rows, NB, PLANE), depth)
    part_a, part_b, part_h = domain(
        got_a, got_b, potential[0], upper[0], slot_owner, slot_row, slot_offset, depth
    )
    grad, ham = scatter(part_a, part_b, part_h.reshape(1, devices, 8, -1), depth)
    return grad.reshape(rows, -1), ham[:rows]


def solution(mesh):
    placed = (
        P(("grp", "dom"), None),
        P("dom", "grp", None),
        P(("grp", "dom"), None),
        P(("grp", "dom")),
        P(("grp", "dom")),
    )
    return jax.shard_map(
        on_device,
        mesh=mesh,
        in_specs=placed,
        out_specs=(P(("grp", "dom"), None), P(("grp", "dom"), None)),
        check_vma=False,
    )
```

```python
import functools

import jax
import jax.numpy as jnp
import numpy as np
from jax import lax
from jax.experimental import pallas as pl
from jax.experimental.pallas import tpu as pltpu
from jax.sharding import PartitionSpec as P

NB = 32
HALF = NB // 2
PLANE = NB * NB
VMEM_LIMIT = 56 * 2**20
MESH = pl.DeviceIdType.MESH
HIGHEST = lax.Precision.HIGHEST


def spline_tables():
    cells_line = np.arange(NB, dtype=np.int32)
    offset = cells_line[:, None] - cells_line[None, :]
    spline = np.where(
        offset == 0, 2.0 / 3.0, np.where(np.abs(offset) == 1, 1.0 / 6.0, 0.0)
    ).astype(np.float32)
    second = np.where(offset == 0, -2.0, np.where(np.abs(offset) == 1, 1.0, 0.0)).astype(np.float32)
    plane_value = np.einsum("ac,bd->abcd", spline, spline).reshape(PLANE, PLANE)
    plane_curve = (
        np.einsum("ac,bd->abcd", second, spline) + np.einsum("ac,bd->abcd", spline, second)
    ).reshape(PLANE, PLANE)
    low = jnp.bfloat16
    return spline.astype(low), second.astype(low), plane_value.astype(low), plane_curve.astype(low)


def passed_along(block, axis, distance):
    devices = range(lax.axis_size(axis))
    route = [((i - distance) % len(devices), i) for i in devices]
    return lax.ppermute(block, axis, route)


def digits(index, depth):
    core = index % 2
    a = (index // 2) % 2
    b = (index // 4) % 2
    z = index // 8
    return z, b, a, core


def place(index, depth, order):
    core, a, b, z = index & 1, (index >> 1) & 1, (index >> 2) & 1, index >> 3
    first, second = (a, b) if order == 0 else (b, a)
    return ((core << 2) + (first << 1) + second) * depth + z


def position(depth):
    me = lax.axis_index("dom")
    z, b, a, core = digits(me, depth)
    to_core = me + 1 - 2 * core
    to_a = me + 2 * (1 - 2 * a)
    to_b = me + 4 * (1 - 2 * b)
    along = [lax.rem(z + dz, depth) for dz in range(1, depth)]
    to_z = [me + 8 * (other - z) for other in along]
    return (z, b, a, core), to_core, to_a, to_b, along, to_z


def meet(partners):
    barrier = pltpu.get_barrier_semaphore()
    for partner in partners:
        pl.semaphore_signal(barrier, inc=1, device_id={"dom": partner}, device_id_type=MESH)
    pl.semaphore_wait(barrier, len(partners))


def gather_kernel(depth, rows, own_ref, got_a, got_b, send, recv, local):
    (z, b, a, core), to_core, to_a, to_b, along, to_z = position(depth)
    meet([to_core, to_a, to_b] + to_z)
    got = (got_a, got_b)
    firsts, seconds = (a, b), (b, a)
    to_first, to_second = (to_a, to_b), (to_b, to_a)

    def remote(src, dst, order, row, phase, target):
        return pltpu.make_async_remote_copy(
            src_ref=src,
            dst_ref=dst,
            send_sem=send.at[order, row, phase],
            recv_sem=recv.at[order, row, phase],
            device_id={"dom": target},
            device_id_type=MESH,
        )

    def base(order):
        return ((core * 2 + firsts[order]) * 2 + seconds[order]) * depth

    own, wide = {}, {}

    def begin(row):
        for order in range(2):
            piece = own_ref.at[row, pl.ds(order * HALF, HALF)]
            spot = got[order].at[row, base(order) + z]
            for dz in range(1, depth):
                copy = remote(piece, spot, order, row, dz - 1, to_z[dz - 1])
                copy.start()
                wide[order, row, dz - 1] = copy
            copy = pltpu.make_async_copy(piece, spot, local.at[order, row])
            copy.start()
            own[order, row] = copy

    def go(order, row, phase):
        if phase == 0:
            if order == 0 and row + 1 < rows:
                begin(row + 1)
            own[order, row].wait()
            for dz in range(1, depth):
                wide[order, row, dz - 1].wait_recv()
            start, size, target = base(order), depth, to_second[order]
        else:
            wide[order, row, depth - 2 + phase].wait_recv()
            if phase == 1:
                start = (core * 2 + firsts[order]) * 2 * depth
                size, target = 2 * depth, to_first[order]
            else:
                start, size, target = core * 4 * depth, 4 * depth, to_core
        block = got[order].at[row, pl.ds(start, size)]
        copy = remote(block, block, order, row, depth - 1 + phase, target)
        copy.start()
        wide[order, row, depth - 1 + phase] = copy

    begin(0)
    for step in range(rows + 2):
        for phase in range(3):
            row = step - phase
            if 0 <= row < rows:
                for order in range(2):
                    go(order, row, phase)
    for row in range(rows):
        for order in range(2):
            wide[order, row, depth + 1].wait_recv()
            for phase in range(depth + 2):
                wide[order, row, phase].wait_send()


def gather(own, depth):
    rows = own.shape[0]
    half = jax.ShapeDtypeStruct((rows, 8 * depth, HALF, PLANE), own.dtype)
    return pl.pallas_call(
        functools.partial(gather_kernel, depth, rows),
        out_shape=(half, half),
        in_specs=[pl.BlockSpec(memory_space=pl.ANY)],
        out_specs=[pl.BlockSpec(memory_space=pl.ANY)] * 2,
        scratch_shapes=[
            pltpu.SemaphoreType.DMA((2, rows, depth + 2)),
            pltpu.SemaphoreType.DMA((2, rows, depth + 2)),
            pltpu.SemaphoreType.DMA((2, rows)),
        ],
        compiler_params=pltpu.CompilerParams(collective_id=0, has_side_effects=True),
    )(own)


def domain_kernel(
    group,
    steps,
    depth,
    owner_of,
    row_of,
    offset_of,
    *refs,
):
    blips_a, blips_b = refs[:group], refs[group : 2 * group]
    (lower, upper, wide_y, back_y, value_ref, curve_ref) = refs[2 * group : 2 * group + 6]
    out_a, out_b, out_h, low_ref, applied_ref, field = refs[2 * group + 6 :]
    step = pl.program_id(0)
    block = group * NB

    @pl.when(step == 0)
    def _():
        count = lower.shape[0]
        field[:count] = lower[...]
        field[count:] = upper[...]
        zero = jnp.zeros((HALF, PLANE), jnp.bfloat16)
        for row in range(out_a.shape[0]):

            @pl.loop(0, out_a.shape[1])
            def _(spot):
                out_a[row, spot] = zero
                out_b[row, spot] = zero

    blips = jnp.concatenate(
        [half[0, 0] for pair in zip(blips_a, blips_b) for half in pair], axis=0
    )
    both = jnp.dot(wide_y[...], blips, preferred_element_type=jnp.float32).astype(jnp.bfloat16)
    y_value, y_curve = both[:block], both[block:]
    value = value_ref[...]
    values_grid = jnp.dot(y_value, value, preferred_element_type=jnp.float32)
    laplace = jnp.dot(y_curve, value, preferred_element_type=jnp.float32) + jnp.dot(
        y_value, curve_ref[...], preferred_element_type=jnp.float32
    )
    cuts = []
    for k in range(group):
        offset = offset_of[step * group + k]
        low_bits = offset & 7
        near = field[pl.ds(pl.multiple_of(offset - low_bits, 8), NB + 8), :]
        cuts.append(pltpu.roll(near, jnp.where(low_bits == 0, 0, NB + 8 - low_bits), 0)[:NB])
    window = jnp.concatenate(cuts, axis=0)
    applied = (-0.5 * laplace + window * values_grid).astype(jnp.bfloat16)
    here = pl.ds(pl.multiple_of(step * block, block), block)
    low_ref[here, :] = values_grid.astype(jnp.bfloat16)
    applied_ref[here, :] = applied
    back_plane = jnp.dot(applied, value, preferred_element_type=jnp.float32).astype(jnp.bfloat16)
    piece = jnp.dot(back_y[...], back_plane, preferred_element_type=jnp.float32).astype(
        jnp.bfloat16
    )
    for k in range(group):
        slot = step * group + k
        for out, order, first in ((out_a, 0, k * NB), (out_b, 1, k * NB + HALF)):
            spot = place(owner_of[slot, 0], depth, order)
            row = row_of[slot]
            total = out[row, spot].astype(jnp.float32) + piece[first : first + HALF].astype(
                jnp.float32
            )
            out[row, spot] = total.astype(jnp.bfloat16)

    @pl.when(step == steps - 1)
    def _():
        gram = lax.dot_general(
            low_ref[...],
            applied_ref[...],
            (((1,), (1,)), ((), ())),
            preferred_element_type=jnp.float32,
        )
        cell_row = lax.broadcasted_iota(jnp.int32, gram.shape, 0) & (NB - 1)
        cell_column = lax.broadcasted_iota(jnp.int32, gram.shape, 1) & (NB - 1)
        terms = jnp.where(cell_row == cell_column, gram, 0.0) / float(NB * PLANE)
        count = gram.shape[0]
        slot = lax.broadcasted_iota(jnp.int32, (1, count), 1) // NB
        hot_row, hot_column = jnp.zeros_like(slot), jnp.zeros_like(slot)
        for k in range(count // NB):
            owner, row = owner_of[k, 0], row_of[k]
            hot_row = jnp.where(slot == k, place(owner, depth, 0) * 8 + row, hot_row)
            hot_column = jnp.where(slot == k, owner * out_a.shape[0] + row, hot_column)
        to_column = (
            hot_column == lax.broadcasted_iota(jnp.int32, (out_h.shape[1], count), 0)
        ).astype(jnp.float32)
        to_row = (
            hot_row == lax.broadcasted_iota(jnp.int32, (out_h.shape[0], count), 0)
        ).astype(jnp.float32)
        by_column = lax.dot_general(
            terms,
            to_column,
            (((1,), (1,)), ((), ())),
            precision=HIGHEST,
            preferred_element_type=jnp.float32,
        )
        out_h[...] = jnp.dot(
            to_row, by_column, precision=HIGHEST, preferred_element_type=jnp.float32
        )


def domain(got_a, got_b, lower, upper, owner, row, offset, depth):
    rows, owners = got_a.shape[:2]
    slots = owner.shape[0]
    group = next(g for g in (8, 6, 4, 3, 2, 1) if slots % g == 0)
    steps = slots // group
    spline, second, plane_value, plane_curve = spline_tables()
    eye = np.eye(group, dtype=np.float32)
    spread = lambda table: np.kron(eye, table.astype(np.float32)).astype(jnp.bfloat16)
    wide_y = np.concatenate([spread(spline), spread(second)], axis=0)
    back_y = spread(spline.T)

    def pick(k, which):
        def index(i, owner_of, row_of, offset_of):
            slot = i * group + k
            return (row_of[slot], place(owner_of[slot, 0], depth, which), 0, 0)

        return pl.BlockSpec((1, 1, HALF, PLANE), index)

    whole = lambda shape: pl.BlockSpec(shape, lambda i, *_: (0,) * len(shape))
    once = lambda shape: pl.BlockSpec(
        shape, lambda i, *_: (0,) * len(shape), pipeline_mode=pl.Buffered(1)
    )
    fixed = (
        lower,
        upper,
        jnp.asarray(wide_y),
        jnp.asarray(back_y),
        jnp.asarray(plane_value),
        jnp.asarray(plane_curve),
    )
    dense = jax.ShapeDtypeStruct((rows, owners, HALF, PLANE), jnp.bfloat16)
    flop = 2 * slots * NB * PLANE * PLANE * 4
    return pl.pallas_call(
        functools.partial(domain_kernel, group, steps, depth),
        grid_spec=pltpu.PrefetchScalarGridSpec(
            num_scalar_prefetch=3,
            grid=(steps,),
            in_specs=[pick(k, 0) for k in range(group)]
            + [pick(k, 1) for k in range(group)]
            + [once(x.shape) for x in fixed],
            out_specs=[whole(dense.shape), whole(dense.shape), whole((owners * 8, owners * rows))],
            scratch_shapes=[
                pltpu.VMEM((slots * NB, PLANE), jnp.bfloat16),
                pltpu.VMEM((slots * NB, PLANE), jnp.bfloat16),
                pltpu.VMEM((2 * lower.shape[0], PLANE), jnp.float32),
            ],
        ),
        out_shape=(
            dense,
            dense,
            jax.ShapeDtypeStruct((owners * 8, owners * rows), jnp.float32),
        ),
        compiler_params=pltpu.CompilerParams(
            vmem_limit_bytes=VMEM_LIMIT, dimension_semantics=("arbitrary",)
        ),
        cost_estimate=pl.CostEstimate(flops=flop, bytes_accessed=2**24, transcendentals=0),
    )(owner, row, offset, *([got_a] * group), *([got_b] * group), *fixed)


def scatter_kernel(depth, rows, part_a, part_b, part_h, grad, ham, *scratch):
    (z, b, a, core), to_core, to_a, to_b, along, to_z = position(depth)
    buffers = (scratch[0:4], scratch[4:8], scratch[8:12])
    send, recv, local = scratch[12:15]
    mine = scratch[15:17]
    held = {}
    for row in range(rows):
        for stream, part in enumerate((part_a, part_b)):
            copy = pltpu.make_async_copy(
                part.at[row, pl.ds(core * 4 * depth, 4 * depth)],
                mine[stream].at[row],
                local.at[stream, row],
            )
            copy.start()
            held[stream, row] = copy
    meet([to_core, to_a, to_b] + to_z)
    parts = (part_a, part_b, part_h)
    firsts, seconds = (a, b, a), (b, a, b)
    to_first, to_second = (to_a, to_b, to_a), (to_b, to_a, to_b)
    flight = {}

    def remote(src, dst, stream, row, phase, target):
        copy = pltpu.make_async_remote_copy(
            src_ref=src,
            dst_ref=dst,
            send_sem=send.at[stream, row, phase],
            recv_sem=recv.at[stream, row, phase],
            device_id={"dom": target},
            device_id_type=MESH,
        )
        copy.start()
        flight[stream, row, phase] = copy

    def add(stream, row, level, source, start, size):
        into = buffers[stream][level]

        @pl.loop(0, size, unroll=2)
        def _(i):
            into[row, i] = into[row, i] + source[row, start + i]

    def go(stream, row, phase):
        first, second, zone, last = buffers[stream]
        part = parts[stream]
        if phase == 0:
            remote(
                part.at[row, pl.ds((1 - core) * 4 * depth, 4 * depth)],
                first.at[row], stream, row, 0, to_core,
            )
        elif phase == 1:
            flight[stream, row, 0].wait_recv()
            if stream == 2:
                add(stream, row, 0, part, core * 4 * depth, 4 * depth)
            else:
                held[stream, row].wait()
                add(stream, row, 0, mine[stream], 0, 4 * depth)
            remote(
                first.at[row, pl.ds((1 - firsts[stream]) * 2 * depth, 2 * depth)],
                second.at[row], stream, row, 1, to_first[stream],
            )
        elif phase == 2:
            flight[stream, row, 1].wait_recv()
            add(stream, row, 1, first, firsts[stream] * 2 * depth, 2 * depth)
            remote(
                second.at[row, pl.ds((1 - seconds[stream]) * depth, depth)],
                zone.at[row], stream, row, 2, to_second[stream],
            )
        elif phase == 3:
            flight[stream, row, 2].wait_recv()
            add(stream, row, 2, second, seconds[stream] * depth, depth)
            for dz in range(1, depth):
                remote(
                    zone.at[row, along[dz - 1]],
                    last.at[row, dz - 1], stream, row, 2 + dz, to_z[dz - 1],
                )
        else:
            for dz in range(1, depth):
                flight[stream, row, 2 + dz].wait_recv()
            total = zone[row, z].astype(jnp.float32)
            for dz in range(1, depth):
                total = total + last[row, dz - 1].astype(jnp.float32)
            if stream == 2:
                ham[...] = total
            else:
                grad[row, stream * HALF : (stream + 1) * HALF, :] = total

    chunks = [[(2, 0), (0, 0), (1, 0)]] + [[(0, row), (1, row)] for row in range(1, rows)]
    for chunk in chunks:
        for stream, row in chunk:
            go(stream, row, 0)
    for step in range(len(chunks) + 3):
        for phase in range(1, 5):
            at = step - (phase - 1)
            if 0 <= at < len(chunks):
                for stream, row in chunks[at]:
                    go(stream, row, phase)
    for copy in flight.values():
        copy.wait_send()


def scatter(part_a, part_b, part_h, depth):
    rows = part_a.shape[0]
    columns = part_h.shape[-1]
    low = lambda count: pltpu.VMEM((rows, count, HALF, PLANE), jnp.bfloat16)
    full = lambda count: pltpu.VMEM((1, count, 8, columns), jnp.float32)
    sizes = (4 * depth, 2 * depth, depth, depth - 1)
    return pl.pallas_call(
        functools.partial(scatter_kernel, depth, rows),
        out_shape=(
            jax.ShapeDtypeStruct((rows, NB, PLANE), jnp.float32),
            jax.ShapeDtypeStruct((8, columns), jnp.float32),
        ),
        in_specs=[pl.BlockSpec(memory_space=pl.ANY)] * 2
        + [pl.BlockSpec(memory_space=pltpu.VMEM)],
        out_specs=[pl.BlockSpec(memory_space=pltpu.VMEM)] * 2,
        scratch_shapes=[low(n) for n in sizes]
        + [low(n) for n in sizes]
        + [full(n) for n in sizes]
        + [
            pltpu.SemaphoreType.DMA((3, rows, depth + 2)),
            pltpu.SemaphoreType.DMA((3, rows, depth + 2)),
            pltpu.SemaphoreType.DMA((2, rows)),
        ]
        + [low(sizes[0])] * 2,
        compiler_params=pltpu.CompilerParams(
            collective_id=1, has_side_effects=True, vmem_limit_bytes=VMEM_LIMIT
        ),
    )(part_a, part_b, part_h)


def on_device(owned_blips, potential, slot_owner, slot_row, slot_offset):
    devices = lax.axis_size("dom")
    depth = devices // 8
    rows = owned_blips.shape[0]
    upper = potential if lax.axis_size("grp") == 1 else passed_along(potential, "grp", -1)
    got_a, got_b = gather(owned_blips.reshape(rows, NB, PLANE), depth)
    part_a, part_b, part_h = domain(
        got_a, got_b, potential[0], upper[0], slot_owner, slot_row, slot_offset, depth
    )
    grad, ham = scatter(part_a, part_b, part_h.reshape(1, devices, 8, -1), depth)
    return grad.reshape(rows, -1), ham[:rows]


def solution(mesh):
    placed = (
        P(("grp", "dom"), None),
        P("dom", "grp", None),
        P(("grp", "dom"), None),
        P(("grp", "dom")),
        P(("grp", "dom")),
    )
    return jax.shard_map(
        on_device,
        mesh=mesh,
        in_specs=placed,
        out_specs=(P(("grp", "dom"), None), P(("grp", "dom"), None)),
        check_vma=False,
    )
```

```python
import functools

import jax
import jax.numpy as jnp
import numpy as np
from jax import lax
from jax.experimental import pallas as pl
from jax.experimental.pallas import tpu as pltpu
from jax.sharding import PartitionSpec as P

NB = 32
HALF = NB // 2
PLANE = NB * NB
VMEM_LIMIT = 56 * 2**20
MESH = pl.DeviceIdType.MESH


def spline_tables():
    cells_line = np.arange(NB, dtype=np.int32)
    offset = cells_line[:, None] - cells_line[None, :]
    spline = np.where(
        offset == 0, 2.0 / 3.0, np.where(np.abs(offset) == 1, 1.0 / 6.0, 0.0)
    ).astype(np.float32)
    second = np.where(offset == 0, -2.0, np.where(np.abs(offset) == 1, 1.0, 0.0)).astype(np.float32)
    plane_value = np.einsum("ac,bd->abcd", spline, spline).reshape(PLANE, PLANE)
    plane_curve = (
        np.einsum("ac,bd->abcd", second, spline) + np.einsum("ac,bd->abcd", spline, second)
    ).reshape(PLANE, PLANE)
    low = jnp.bfloat16
    return spline.astype(low), second.astype(low), plane_value.astype(low), plane_curve.astype(low)


def passed_along(block, axis, distance):
    devices = range(lax.axis_size(axis))
    route = [((i - distance) % len(devices), i) for i in devices]
    return lax.ppermute(block, axis, route)


def digits(index, depth):
    core = index % 2
    a = (index // 2) % 2
    b = (index // 4) % 2
    z = index // 8
    return z, b, a, core


def place(index, depth, order):
    core, a, b, z = index & 1, (index >> 1) & 1, (index >> 2) & 1, index >> 3
    first, second = (a, b) if order == 0 else (b, a)
    return ((core << 2) + (first << 1) + second) * depth + z


def position(depth):
    me = lax.axis_index("dom")
    z, b, a, core = digits(me, depth)
    to_core = me + 1 - 2 * core
    to_a = me + 2 * (1 - 2 * a)
    to_b = me + 4 * (1 - 2 * b)
    along = [lax.rem(z + dz, depth) for dz in range(1, depth)]
    to_z = [me + 8 * (other - z) for other in along]
    return (z, b, a, core), to_core, to_a, to_b, along, to_z


def meet(partners):
    barrier = pltpu.get_barrier_semaphore()
    for partner in partners:
        pl.semaphore_signal(barrier, inc=1, device_id={"dom": partner}, device_id_type=MESH)
    pl.semaphore_wait(barrier, len(partners))


def gather_kernel(depth, rows, own_ref, got_a, got_b, send, recv, local):
    (z, b, a, core), to_core, to_a, to_b, along, to_z = position(depth)
    meet([to_core, to_a, to_b] + to_z)
    got = (got_a, got_b)
    firsts, seconds = (a, b), (b, a)
    to_first, to_second = (to_a, to_b), (to_b, to_a)

    def remote(src, dst, order, row, phase, target):
        return pltpu.make_async_remote_copy(
            src_ref=src,
            dst_ref=dst,
            send_sem=send.at[order, row, phase],
            recv_sem=recv.at[order, row, phase],
            device_id={"dom": target},
            device_id_type=MESH,
        )

    def base(order):
        return ((core * 2 + firsts[order]) * 2 + seconds[order]) * depth

    own, wide = {}, {}

    def begin(row):
        for order in range(2):
            piece = own_ref.at[row, pl.ds(order * HALF, HALF)]
            spot = got[order].at[row, base(order) + z]
            for dz in range(1, depth):
                copy = remote(piece, spot, order, row, dz - 1, to_z[dz - 1])
                copy.start()
                wide[order, row, dz - 1] = copy
            copy = pltpu.make_async_copy(piece, spot, local.at[order, row])
            copy.start()
            own[order, row] = copy

    def go(order, row, phase):
        if phase == 0:
            if order == 0 and row + 1 < rows:
                begin(row + 1)
            own[order, row].wait()
            for dz in range(1, depth):
                wide[order, row, dz - 1].wait_recv()
            start, size, target = base(order), depth, to_second[order]
        else:
            wide[order, row, depth - 2 + phase].wait_recv()
            if phase == 1:
                start = (core * 2 + firsts[order]) * 2 * depth
                size, target = 2 * depth, to_first[order]
            else:
                start, size, target = core * 4 * depth, 4 * depth, to_core
        block = got[order].at[row, pl.ds(start, size)]
        copy = remote(block, block, order, row, depth - 1 + phase, target)
        copy.start()
        wide[order, row, depth - 1 + phase] = copy

    begin(0)
    for step in range(rows + 2):
        for phase in range(3):
            row = step - phase
            if 0 <= row < rows:
                for order in range(2):
                    go(order, row, phase)
    for row in range(rows):
        for order in range(2):
            wide[order, row, depth + 1].wait_recv()
            for phase in range(depth + 2):
                wide[order, row, phase].wait_send()


def gather(own, depth):
    rows = own.shape[0]
    half = jax.ShapeDtypeStruct((rows, 8 * depth, HALF, PLANE), own.dtype)
    return pl.pallas_call(
        functools.partial(gather_kernel, depth, rows),
        out_shape=(half, half),
        in_specs=[pl.BlockSpec(memory_space=pl.ANY)],
        out_specs=[pl.BlockSpec(memory_space=pl.ANY)] * 2,
        scratch_shapes=[
            pltpu.SemaphoreType.DMA((2, rows, depth + 2)),
            pltpu.SemaphoreType.DMA((2, rows, depth + 2)),
            pltpu.SemaphoreType.DMA((2, rows)),
        ],
        compiler_params=pltpu.CompilerParams(collective_id=0, has_side_effects=True),
    )(own)


def split(wide):
    high = wide.astype(jnp.bfloat16)
    rest = wide - high.astype(jnp.float32)
    middle = rest.astype(jnp.bfloat16)
    return high, middle, (rest - middle.astype(jnp.float32)).astype(jnp.bfloat16)


def domain_kernel(
    group,
    steps,
    depth,
    owner_of,
    row_of,
    offset_of,
    *refs,
):
    blips_a, blips_b = refs[:group], refs[group : 2 * group]
    (lower, upper, wide_y, back_y, value_ref, curve_ref) = refs[2 * group : 2 * group + 6]
    out_a, out_b, out_h, low_ref, applied_ref, field = refs[2 * group + 6 :]
    step = pl.program_id(0)
    block = group * NB

    @pl.when(step == 0)
    def _():
        count = lower.shape[0]
        field[:count] = lower[...]
        field[count:] = upper[...]
        zero = jnp.zeros((HALF, PLANE), jnp.bfloat16)
        for row in range(out_a.shape[0]):

            @pl.loop(0, out_a.shape[1], unroll=4)
            def _(spot):
                out_a[row, spot] = zero
                out_b[row, spot] = zero

    blips = jnp.concatenate(
        [half[0, 0] for pair in zip(blips_a, blips_b) for half in pair], axis=0
    )
    both = jnp.dot(wide_y[...], blips, preferred_element_type=jnp.float32).astype(jnp.bfloat16)
    y_value, y_curve = both[:block], both[block:]
    value = value_ref[...]
    values_grid = jnp.dot(y_value, value, preferred_element_type=jnp.float32)
    laplace = jnp.dot(y_curve, value, preferred_element_type=jnp.float32) + jnp.dot(
        y_value, curve_ref[...], preferred_element_type=jnp.float32
    )
    cuts = []
    for k in range(group):
        offset = offset_of[step * group + k]
        low_bits = offset & 7
        near = field[pl.ds(pl.multiple_of(offset - low_bits, 8), NB + 8), :]
        cuts.append(pltpu.roll(near, jnp.where(low_bits == 0, 0, NB + 8 - low_bits), 0)[:NB])
    window = jnp.concatenate(cuts, axis=0)
    applied = (-0.5 * laplace + window * values_grid).astype(jnp.bfloat16)
    here = pl.ds(pl.multiple_of(step * block, block), block)
    low_ref[here, :] = values_grid.astype(jnp.bfloat16)
    applied_ref[here, :] = applied
    back_plane = jnp.dot(applied, value, preferred_element_type=jnp.float32).astype(jnp.bfloat16)
    piece = jnp.dot(back_y[...], back_plane, preferred_element_type=jnp.float32).astype(
        jnp.bfloat16
    )
    for k in range(group):
        slot = step * group + k
        for out, order, first in ((out_a, 0, k * NB), (out_b, 1, k * NB + HALF)):
            spot = place(owner_of[slot, 0], depth, order)
            row = row_of[slot]
            total = out[row, spot].astype(jnp.float32) + piece[first : first + HALF].astype(
                jnp.float32
            )
            out[row, spot] = total.astype(jnp.bfloat16)

    @pl.when(step == steps - 1)
    def _():
        gram = lax.dot_general(
            low_ref[...],
            applied_ref[...],
            (((1,), (1,)), ((), ())),
            preferred_element_type=jnp.float32,
        )
        cell_row = lax.broadcasted_iota(jnp.int32, gram.shape, 0) & (NB - 1)
        cell_column = lax.broadcasted_iota(jnp.int32, gram.shape, 1) & (NB - 1)
        terms = jnp.where(cell_row == cell_column, gram, 0.0) / float(NB * PLANE)
        count = gram.shape[0]
        slot = lax.broadcasted_iota(jnp.int32, (1, count), 1) // NB
        hot_row, hot_column = jnp.zeros_like(slot), jnp.zeros_like(slot)
        for k in range(count // NB):
            owner, row = owner_of[k, 0], row_of[k]
            hot_row = jnp.where(slot == k, place(owner, depth, 0) * 8 + row, hot_row)
            hot_column = jnp.where(slot == k, owner * out_a.shape[0] + row, hot_column)
        to_column = jnp.where(
            hot_column == lax.broadcasted_iota(jnp.int32, (out_h.shape[1], count), 0), 1.0, 0.0
        ).astype(jnp.bfloat16)
        to_row = jnp.where(
            hot_row == lax.broadcasted_iota(jnp.int32, (out_h.shape[0], count), 0), 1.0, 0.0
        ).astype(jnp.bfloat16)
        by_column = 0.0
        for part in split(terms):
            by_column += lax.dot_general(
                part, to_column, (((1,), (1,)), ((), ())), preferred_element_type=jnp.float32
            )
        total = 0.0
        for part in split(by_column):
            total += jnp.dot(to_row, part, preferred_element_type=jnp.float32)
        out_h[...] = total


def domain(got_a, got_b, lower, upper, owner, row, offset, depth):
    rows, owners = got_a.shape[:2]
    slots = owner.shape[0]
    group = next(g for g in (8, 6, 4, 3, 2, 1) if slots % g == 0)
    steps = slots // group
    spline, second, plane_value, plane_curve = spline_tables()
    eye = np.eye(group, dtype=np.float32)
    spread = lambda table: np.kron(eye, table.astype(np.float32)).astype(jnp.bfloat16)
    wide_y = np.concatenate([spread(spline), spread(second)], axis=0)
    back_y = spread(spline.T)

    def pick(k, which):
        def index(i, owner_of, row_of, offset_of):
            slot = i * group + k
            return (row_of[slot], place(owner_of[slot, 0], depth, which), 0, 0)

        return pl.BlockSpec((1, 1, HALF, PLANE), index)

    whole = lambda shape: pl.BlockSpec(shape, lambda i, *_: (0,) * len(shape))
    once = lambda shape: pl.BlockSpec(
        shape, lambda i, *_: (0,) * len(shape), pipeline_mode=pl.Buffered(1)
    )
    fixed = (
        lower,
        upper,
        jnp.asarray(wide_y),
        jnp.asarray(back_y),
        jnp.asarray(plane_value),
        jnp.asarray(plane_curve),
    )
    dense = jax.ShapeDtypeStruct((rows, owners, HALF, PLANE), jnp.bfloat16)
    flop = 2 * slots * NB * PLANE * PLANE * 4
    return pl.pallas_call(
        functools.partial(domain_kernel, group, steps, depth),
        grid_spec=pltpu.PrefetchScalarGridSpec(
            num_scalar_prefetch=3,
            grid=(steps,),
            in_specs=[pick(k, 0) for k in range(group)]
            + [pick(k, 1) for k in range(group)]
            + [once(x.shape) for x in fixed],
            out_specs=[whole(dense.shape), whole(dense.shape), whole((owners * 8, owners * rows))],
            scratch_shapes=[
                pltpu.VMEM((slots * NB, PLANE), jnp.bfloat16),
                pltpu.VMEM((slots * NB, PLANE), jnp.bfloat16),
                pltpu.VMEM((2 * lower.shape[0], PLANE), jnp.float32),
            ],
        ),
        out_shape=(
            dense,
            dense,
            jax.ShapeDtypeStruct((owners * 8, owners * rows), jnp.float32),
        ),
        compiler_params=pltpu.CompilerParams(
            vmem_limit_bytes=VMEM_LIMIT, dimension_semantics=("arbitrary",)
        ),
        cost_estimate=pl.CostEstimate(flops=flop, bytes_accessed=2**24, transcendentals=0),
    )(owner, row, offset, *([got_a] * group), *([got_b] * group), *fixed)


def scatter_kernel(depth, rows, part_a, part_b, part_h, grad, ham, *scratch):
    (z, b, a, core), to_core, to_a, to_b, along, to_z = position(depth)
    buffers = (scratch[0:4], scratch[4:8], scratch[8:12])
    send, recv, local = scratch[12:15]
    mine = scratch[15:17]
    held = {}
    for row in range(rows):
        for stream, part in enumerate((part_a, part_b)):
            copy = pltpu.make_async_copy(
                part.at[row, pl.ds(core * 4 * depth, 4 * depth)],
                mine[stream].at[row],
                local.at[stream, row],
            )
            copy.start()
            held[stream, row] = copy
    meet([to_core, to_a, to_b] + to_z)
    parts = (part_a, part_b, part_h)
    firsts, seconds = (a, b, a), (b, a, b)
    to_first, to_second = (to_a, to_b, to_a), (to_b, to_a, to_b)
    flight = {}

    def remote(src, dst, stream, row, phase, target):
        copy = pltpu.make_async_remote_copy(
            src_ref=src,
            dst_ref=dst,
            send_sem=send.at[stream, row, phase],
            recv_sem=recv.at[stream, row, phase],
            device_id={"dom": target},
            device_id_type=MESH,
        )
        copy.start()
        flight[stream, row, phase] = copy

    def add(stream, row, level, source, start, size):
        into = buffers[stream][level]

        @pl.loop(0, size, unroll=2)
        def _(i):
            into[row, i] = into[row, i] + source[row, start + i]

    def go(stream, row, phase):
        first, second, zone, last = buffers[stream]
        part = parts[stream]
        if phase == 0:
            remote(
                part.at[row, pl.ds((1 - core) * 4 * depth, 4 * depth)],
                first.at[row], stream, row, 0, to_core,
            )
        elif phase == 1:
            flight[stream, row, 0].wait_recv()
            if stream == 2:
                add(stream, row, 0, part, core * 4 * depth, 4 * depth)
            else:
                held[stream, row].wait()
                add(stream, row, 0, mine[stream], 0, 4 * depth)
            remote(
                first.at[row, pl.ds((1 - firsts[stream]) * 2 * depth, 2 * depth)],
                second.at[row], stream, row, 1, to_first[stream],
            )
        elif phase == 2:
            flight[stream, row, 1].wait_recv()
            add(stream, row, 1, first, firsts[stream] * 2 * depth, 2 * depth)
            remote(
                second.at[row, pl.ds((1 - seconds[stream]) * depth, depth)],
                zone.at[row], stream, row, 2, to_second[stream],
            )
        elif phase == 3:
            flight[stream, row, 2].wait_recv()
            add(stream, row, 2, second, seconds[stream] * depth, depth)
            for dz in range(1, depth):
                remote(
                    zone.at[row, along[dz - 1]],
                    last.at[row, dz - 1], stream, row, 2 + dz, to_z[dz - 1],
                )
        else:
            for dz in range(1, depth):
                flight[stream, row, 2 + dz].wait_recv()
            total = zone[row, z].astype(jnp.float32)
            for dz in range(1, depth):
                total = total + last[row, dz - 1].astype(jnp.float32)
            if stream == 2:
                ham[...] = total
            else:
                grad[row, stream * HALF : (stream + 1) * HALF, :] = total

    chunks = [[(2, 0), (0, 0), (1, 0)]] + [[(0, row), (1, row)] for row in range(1, rows)]
    for chunk in chunks:
        for stream, row in chunk:
            go(stream, row, 0)
    for step in range(len(chunks) + 3):
        for phase in range(1, 5):
            at = step - (phase - 1)
            if 0 <= at < len(chunks):
                for stream, row in chunks[at]:
                    go(stream, row, phase)
    for copy in flight.values():
        copy.wait_send()


def scatter(part_a, part_b, part_h, depth):
    rows = part_a.shape[0]
    columns = part_h.shape[-1]
    low = lambda count: pltpu.VMEM((rows, count, HALF, PLANE), jnp.bfloat16)
    full = lambda count: pltpu.VMEM((1, count, 8, columns), jnp.float32)
    sizes = (4 * depth, 2 * depth, depth, depth - 1)
    return pl.pallas_call(
        functools.partial(scatter_kernel, depth, rows),
        out_shape=(
            jax.ShapeDtypeStruct((rows, NB, PLANE), jnp.float32),
            jax.ShapeDtypeStruct((8, columns), jnp.float32),
        ),
        in_specs=[pl.BlockSpec(memory_space=pl.ANY)] * 2
        + [pl.BlockSpec(memory_space=pltpu.VMEM)],
        out_specs=[pl.BlockSpec(memory_space=pltpu.VMEM)] * 2,
        scratch_shapes=[low(n) for n in sizes]
        + [low(n) for n in sizes]
        + [full(n) for n in sizes]
        + [
            pltpu.SemaphoreType.DMA((3, rows, depth + 2)),
            pltpu.SemaphoreType.DMA((3, rows, depth + 2)),
            pltpu.SemaphoreType.DMA((2, rows)),
        ]
        + [low(sizes[0])] * 2,
        compiler_params=pltpu.CompilerParams(
            collective_id=1, has_side_effects=True, vmem_limit_bytes=VMEM_LIMIT
        ),
    )(part_a, part_b, part_h)


def on_device(owned_blips, potential, slot_owner, slot_row, slot_offset):
    devices = lax.axis_size("dom")
    depth = devices // 8
    rows = owned_blips.shape[0]
    upper = potential if lax.axis_size("grp") == 1 else passed_along(potential, "grp", -1)
    got_a, got_b = gather(owned_blips.reshape(rows, NB, PLANE), depth)
    part_a, part_b, part_h = domain(
        got_a, got_b, potential[0], upper[0], slot_owner, slot_row, slot_offset, depth
    )
    grad, ham = scatter(part_a, part_b, part_h.reshape(1, devices, 8, -1), depth)
    return grad.reshape(rows, -1), ham[:rows]


def solution(mesh):
    placed = (
        P(("grp", "dom"), None),
        P("dom", "grp", None),
        P(("grp", "dom"), None),
        P(("grp", "dom")),
        P(("grp", "dom")),
    )
    return jax.shard_map(
        on_device,
        mesh=mesh,
        in_specs=placed,
        out_specs=(P(("grp", "dom"), None), P(("grp", "dom"), None)),
        check_vma=False,
    )
```

```python
import functools

import jax
import jax.numpy as jnp
import numpy as np
from jax import lax
from jax.experimental import pallas as pl
from jax.experimental.pallas import tpu as pltpu
from jax.sharding import PartitionSpec as P

NB = 32
HALF = NB // 2
PLANE = NB * NB
VMEM_LIMIT = 56 * 2**20
MESH = pl.DeviceIdType.MESH


def spline_tables():
    cells_line = np.arange(NB, dtype=np.int32)
    offset = cells_line[:, None] - cells_line[None, :]
    spline = np.where(
        offset == 0, 2.0 / 3.0, np.where(np.abs(offset) == 1, 1.0 / 6.0, 0.0)
    ).astype(np.float32)
    second = np.where(offset == 0, -2.0, np.where(np.abs(offset) == 1, 1.0, 0.0)).astype(np.float32)
    plane_value = np.einsum("ac,bd->abcd", spline, spline).reshape(PLANE, PLANE)
    plane_curve = (
        np.einsum("ac,bd->abcd", second, spline) + np.einsum("ac,bd->abcd", spline, second)
    ).reshape(PLANE, PLANE)
    low = jnp.bfloat16
    return spline.astype(low), second.astype(low), plane_value.astype(low), plane_curve.astype(low)


def passed_along(block, axis, distance):
    devices = range(lax.axis_size(axis))
    route = [((i - distance) % len(devices), i) for i in devices]
    return lax.ppermute(block, axis, route)


def digits(index, depth):
    core = index % 2
    a = (index // 2) % 2
    b = (index // 4) % 2
    z = index // 8
    return z, b, a, core


def place(index, depth, order):
    core, a, b, z = index & 1, (index >> 1) & 1, (index >> 2) & 1, index >> 3
    first, second = (a, b) if order == 0 else (b, a)
    return ((core << 2) + (first << 1) + second) * depth + z


def position(depth):
    me = lax.axis_index("dom")
    z, b, a, core = digits(me, depth)
    to_core = me + 1 - 2 * core
    to_a = me + 2 * (1 - 2 * a)
    to_b = me + 4 * (1 - 2 * b)
    along = [lax.rem(z + dz, depth) for dz in range(1, depth)]
    to_z = [me + 8 * (other - z) for other in along]
    return (z, b, a, core), to_core, to_a, to_b, along, to_z


def meet(partners):
    barrier = pltpu.get_barrier_semaphore()
    for partner in partners:
        pl.semaphore_signal(barrier, inc=1, device_id={"dom": partner}, device_id_type=MESH)
    pl.semaphore_wait(barrier, len(partners))


def gather_kernel(depth, rows, own_ref, got_a, got_b, send, recv, local):
    (z, b, a, core), to_core, to_a, to_b, along, to_z = position(depth)
    meet([to_core, to_a, to_b] + to_z)
    got = (got_a, got_b)
    firsts, seconds = (a, b), (b, a)
    to_first, to_second = (to_a, to_b), (to_b, to_a)

    def remote(src, dst, order, row, phase, target):
        return pltpu.make_async_remote_copy(
            src_ref=src,
            dst_ref=dst,
            send_sem=send.at[order, row, phase],
            recv_sem=recv.at[order, row, phase],
            device_id={"dom": target},
            device_id_type=MESH,
        )

    def base(order):
        return ((core * 2 + firsts[order]) * 2 + seconds[order]) * depth

    own, wide = {}, {}

    def begin(row):
        for order in range(2):
            piece = own_ref.at[row, pl.ds(order * HALF, HALF)]
            spot = got[order].at[row, base(order) + z]
            for dz in range(1, depth):
                copy = remote(piece, spot, order, row, dz - 1, to_z[dz - 1])
                copy.start()
                wide[order, row, dz - 1] = copy
            copy = pltpu.make_async_copy(piece, spot, local.at[order, row])
            copy.start()
            own[order, row] = copy

    def go(order, row, phase):
        if phase == 0:
            if order == 0 and row + 1 < rows:
                begin(row + 1)
            own[order, row].wait()
            for dz in range(1, depth):
                wide[order, row, dz - 1].wait_recv()
            start, size, target = base(order), depth, to_second[order]
        else:
            wide[order, row, depth - 2 + phase].wait_recv()
            if phase == 1:
                start = (core * 2 + firsts[order]) * 2 * depth
                size, target = 2 * depth, to_first[order]
            else:
                start, size, target = core * 4 * depth, 4 * depth, to_core
        block = got[order].at[row, pl.ds(start, size)]
        copy = remote(block, block, order, row, depth - 1 + phase, target)
        copy.start()
        wide[order, row, depth - 1 + phase] = copy

    begin(0)
    for step in range(rows + 2):
        for phase in range(3):
            row = step - phase
            if 0 <= row < rows:
                for order in range(2):
                    go(order, row, phase)
    for row in range(rows):
        for order in range(2):
            wide[order, row, depth + 1].wait_recv()
            for phase in range(depth + 2):
                wide[order, row, phase].wait_send()


def gather(own, depth):
    rows = own.shape[0]
    half = jax.ShapeDtypeStruct((rows, 8 * depth, HALF, PLANE), own.dtype)
    return pl.pallas_call(
        functools.partial(gather_kernel, depth, rows),
        out_shape=(half, half),
        in_specs=[pl.BlockSpec(memory_space=pl.ANY)],
        out_specs=[pl.BlockSpec(memory_space=pl.ANY)] * 2,
        scratch_shapes=[
            pltpu.SemaphoreType.DMA((2, rows, depth + 2)),
            pltpu.SemaphoreType.DMA((2, rows, depth + 2)),
            pltpu.SemaphoreType.DMA((2, rows)),
        ],
        compiler_params=pltpu.CompilerParams(collective_id=0, has_side_effects=True),
    )(own)


def split(wide):
    high = wide.astype(jnp.bfloat16)
    rest = wide - high.astype(jnp.float32)
    middle = rest.astype(jnp.bfloat16)
    return high, middle, (rest - middle.astype(jnp.float32)).astype(jnp.bfloat16)


def domain_kernel(
    group,
    steps,
    depth,
    owner_of,
    row_of,
    offset_of,
    *refs,
):
    blips_a, blips_b = refs[:group], refs[group : 2 * group]
    (lower, upper, wide_y, back_y, value_ref, curve_ref) = refs[2 * group : 2 * group + 6]
    out_a, out_b, out_h, low_ref, applied_ref, field = refs[2 * group + 6 :]
    step = pl.program_id(0)
    block = group * NB

    @pl.when(step == 0)
    def _():
        count = lower.shape[0]
        field[:count] = lower[...]
        field[count:] = upper[...]
        zero = jnp.zeros((HALF, PLANE), jnp.bfloat16)
        for row in range(out_a.shape[0]):

            @pl.loop(0, out_a.shape[1], unroll=4)
            def _(spot):
                out_a[row, spot] = zero
                out_b[row, spot] = zero

    blips = jnp.concatenate(
        [half[0, 0] for pair in zip(blips_a, blips_b) for half in pair], axis=0
    )
    both = jnp.dot(wide_y[...], blips, preferred_element_type=jnp.float32).astype(jnp.bfloat16)
    y_value, y_curve = both[:block], both[block:]
    value = value_ref[...]
    values_grid = jnp.dot(y_value, value, preferred_element_type=jnp.float32)
    laplace = jnp.dot(y_curve, value, preferred_element_type=jnp.float32) + jnp.dot(
        y_value, curve_ref[...], preferred_element_type=jnp.float32
    )
    cuts = []
    for k in range(group):
        offset = offset_of[step * group + k]
        low_bits = offset & 7
        near = field[pl.ds(pl.multiple_of(offset - low_bits, 8), NB + 8), :]
        cuts.append(pltpu.roll(near, jnp.where(low_bits == 0, 0, NB + 8 - low_bits), 0)[:NB])
    window = jnp.concatenate(cuts, axis=0)
    applied = (-0.5 * laplace + window * values_grid).astype(jnp.bfloat16)
    here = pl.ds(pl.multiple_of(step * block, block), block)
    low_ref[here, :] = values_grid.astype(jnp.bfloat16)
    applied_ref[here, :] = applied
    back_plane = jnp.dot(applied, value, preferred_element_type=jnp.float32).astype(jnp.bfloat16)
    piece = jnp.dot(back_y[...], back_plane, preferred_element_type=jnp.float32).astype(
        jnp.bfloat16
    )
    for k in range(group):
        slot = step * group + k
        for out, order, first in ((out_a, 0, k * NB), (out_b, 1, k * NB + HALF)):
            spot = place(owner_of[slot], depth, order)
            row = row_of[slot]
            total = out[row, spot].astype(jnp.float32) + piece[first : first + HALF].astype(
                jnp.float32
            )
            out[row, spot] = total.astype(jnp.bfloat16)

    @pl.when(step == steps - 1)
    def _():
        gram = lax.dot_general(
            low_ref[...],
            applied_ref[...],
            (((1,), (1,)), ((), ())),
            preferred_element_type=jnp.float32,
        )
        cell_row = lax.broadcasted_iota(jnp.int32, gram.shape, 0) & (NB - 1)
        cell_column = lax.broadcasted_iota(jnp.int32, gram.shape, 1) & (NB - 1)
        terms = jnp.where(cell_row == cell_column, gram, 0.0) / float(NB * PLANE)
        count = gram.shape[0]
        slot = lax.broadcasted_iota(jnp.int32, (1, count), 1) // NB
        hot_row, hot_column = jnp.zeros_like(slot), jnp.zeros_like(slot)
        for k in range(count // NB):
            owner, row = owner_of[k], row_of[k]
            hot_row = jnp.where(slot == k, place(owner, depth, 0) * 8 + row, hot_row)
            hot_column = jnp.where(slot == k, owner * out_a.shape[0] + row, hot_column)
        to_column = jnp.where(
            hot_column == lax.broadcasted_iota(jnp.int32, (out_h.shape[1], count), 0), 1.0, 0.0
        ).astype(jnp.bfloat16)
        to_row = jnp.where(
            hot_row == lax.broadcasted_iota(jnp.int32, (out_h.shape[0], count), 0), 1.0, 0.0
        ).astype(jnp.bfloat16)
        by_column = 0.0
        for part in split(terms):
            by_column += lax.dot_general(
                part, to_column, (((1,), (1,)), ((), ())), preferred_element_type=jnp.float32
            )
        total = 0.0
        for part in split(by_column):
            total += jnp.dot(to_row, part, preferred_element_type=jnp.float32)
        out_h[...] = total


def domain(got_a, got_b, lower, upper, owner, row, offset, depth):
    rows, owners = got_a.shape[:2]
    slots = owner.shape[0]
    group = next(g for g in (8, 6, 4, 3, 2, 1) if slots % g == 0)
    steps = slots // group
    spline, second, plane_value, plane_curve = spline_tables()
    eye = np.eye(group, dtype=np.float32)
    spread = lambda table: np.kron(eye, table.astype(np.float32)).astype(jnp.bfloat16)
    wide_y = np.concatenate([spread(spline), spread(second)], axis=0)
    back_y = spread(spline.T)

    def pick(k, which):
        def index(i, owner_of, row_of, offset_of):
            slot = i * group + k
            return (row_of[slot], place(owner_of[slot], depth, which), 0, 0)

        return pl.BlockSpec((1, 1, HALF, PLANE), index)

    whole = lambda shape: pl.BlockSpec(shape, lambda i, *_: (0,) * len(shape))
    once = lambda shape: pl.BlockSpec(
        shape, lambda i, *_: (0,) * len(shape), pipeline_mode=pl.Buffered(1)
    )
    fixed = (
        lower,
        upper,
        jnp.asarray(wide_y),
        jnp.asarray(back_y),
        jnp.asarray(plane_value),
        jnp.asarray(plane_curve),
    )
    dense = jax.ShapeDtypeStruct((rows, owners, HALF, PLANE), jnp.bfloat16)
    flop = 2 * slots * NB * PLANE * PLANE * 4
    return pl.pallas_call(
        functools.partial(domain_kernel, group, steps, depth),
        grid_spec=pltpu.PrefetchScalarGridSpec(
            num_scalar_prefetch=3,
            grid=(steps,),
            in_specs=[pick(k, 0) for k in range(group)]
            + [pick(k, 1) for k in range(group)]
            + [once(x.shape) for x in fixed],
            out_specs=[whole(dense.shape), whole(dense.shape), whole((owners * 8, owners * rows))],
            scratch_shapes=[
                pltpu.VMEM((slots * NB, PLANE), jnp.bfloat16),
                pltpu.VMEM((slots * NB, PLANE), jnp.bfloat16),
                pltpu.VMEM((2 * lower.shape[0], PLANE), jnp.float32),
            ],
        ),
        out_shape=(
            dense,
            dense,
            jax.ShapeDtypeStruct((owners * 8, owners * rows), jnp.float32),
        ),
        compiler_params=pltpu.CompilerParams(
            vmem_limit_bytes=VMEM_LIMIT, dimension_semantics=("arbitrary",)
        ),
        cost_estimate=pl.CostEstimate(flops=flop, bytes_accessed=2**24, transcendentals=0),
    )(owner, row, offset, *([got_a] * group), *([got_b] * group), *fixed)


def scatter_kernel(depth, rows, part_a, part_b, part_h, grad, ham, *scratch):
    (z, b, a, core), to_core, to_a, to_b, along, to_z = position(depth)
    buffers = (scratch[0:4], scratch[4:8], scratch[8:12])
    send, recv, local = scratch[12:15]
    mine = scratch[15:17]
    held = {}
    for row in range(rows):
        for stream, part in enumerate((part_a, part_b)):
            copy = pltpu.make_async_copy(
                part.at[row, pl.ds(core * 4 * depth, 4 * depth)],
                mine[stream].at[row],
                local.at[stream, row],
            )
            copy.start()
            held[stream, row] = copy
    meet([to_core, to_a, to_b] + to_z)
    parts = (part_a, part_b, part_h)
    firsts, seconds = (a, b, a), (b, a, b)
    to_first, to_second = (to_a, to_b, to_a), (to_b, to_a, to_b)
    flight = {}

    def remote(src, dst, stream, row, phase, target):
        copy = pltpu.make_async_remote_copy(
            src_ref=src,
            dst_ref=dst,
            send_sem=send.at[stream, row, phase],
            recv_sem=recv.at[stream, row, phase],
            device_id={"dom": target},
            device_id_type=MESH,
        )
        copy.start()
        flight[stream, row, phase] = copy

    def add(stream, row, level, source, start, size):
        into = buffers[stream][level]

        @pl.loop(0, size, unroll=2)
        def _(i):
            into[row, i] = into[row, i] + source[row, start + i]

    def go(stream, row, phase):
        first, second, zone, last = buffers[stream]
        part = parts[stream]
        if phase == 0:
            remote(
                part.at[row, pl.ds((1 - core) * 4 * depth, 4 * depth)],
                first.at[row], stream, row, 0, to_core,
            )
        elif phase == 1:
            flight[stream, row, 0].wait_recv()
            if stream == 2:
                add(stream, row, 0, part, core * 4 * depth, 4 * depth)
            else:
                held[stream, row].wait()
                add(stream, row, 0, mine[stream], 0, 4 * depth)
            remote(
                first.at[row, pl.ds((1 - firsts[stream]) * 2 * depth, 2 * depth)],
                second.at[row], stream, row, 1, to_first[stream],
            )
        elif phase == 2:
            flight[stream, row, 1].wait_recv()
            add(stream, row, 1, first, firsts[stream] * 2 * depth, 2 * depth)
            remote(
                second.at[row, pl.ds((1 - seconds[stream]) * depth, depth)],
                zone.at[row], stream, row, 2, to_second[stream],
            )
        elif phase == 3:
            flight[stream, row, 2].wait_recv()
            add(stream, row, 2, second, seconds[stream] * depth, depth)
            for dz in range(1, depth):
                remote(
                    zone.at[row, along[dz - 1]],
                    last.at[row, dz - 1], stream, row, 2 + dz, to_z[dz - 1],
                )
        else:
            for dz in range(1, depth):
                flight[stream, row, 2 + dz].wait_recv()
            total = zone[row, z].astype(jnp.float32)
            for dz in range(1, depth):
                total = total + last[row, dz - 1].astype(jnp.float32)
            if stream == 2:
                ham[...] = total[:rows]
            else:
                grad[row, stream * HALF : (stream + 1) * HALF, :] = total

    chunks = [[(2, 0), (0, 0), (1, 0)]] + [[(0, row), (1, row)] for row in range(1, rows)]
    for chunk in chunks:
        for stream, row in chunk:
            go(stream, row, 0)
    for step in range(len(chunks) + 3):
        for phase in range(1, 5):
            at = step - (phase - 1)
            if 0 <= at < len(chunks):
                for stream, row in chunks[at]:
                    go(stream, row, phase)
    for copy in flight.values():
        copy.wait_send()


def scatter(part_a, part_b, part_h, depth):
    rows = part_a.shape[0]
    columns = part_h.shape[-1]
    low = lambda count: pltpu.VMEM((rows, count, HALF, PLANE), jnp.bfloat16)
    full = lambda count: pltpu.VMEM((1, count, 8, columns), jnp.float32)
    sizes = (4 * depth, 2 * depth, depth, depth - 1)
    return pl.pallas_call(
        functools.partial(scatter_kernel, depth, rows),
        out_shape=(
            jax.ShapeDtypeStruct((rows, NB, PLANE), jnp.float32),
            jax.ShapeDtypeStruct((rows, columns), jnp.float32),
        ),
        in_specs=[pl.BlockSpec(memory_space=pl.ANY)] * 2
        + [pl.BlockSpec(memory_space=pltpu.VMEM)],
        out_specs=[pl.BlockSpec(memory_space=pltpu.VMEM)] * 2,
        scratch_shapes=[low(n) for n in sizes]
        + [low(n) for n in sizes]
        + [full(n) for n in sizes]
        + [
            pltpu.SemaphoreType.DMA((3, rows, depth + 2)),
            pltpu.SemaphoreType.DMA((3, rows, depth + 2)),
            pltpu.SemaphoreType.DMA((2, rows)),
        ]
        + [low(sizes[0])] * 2,
        compiler_params=pltpu.CompilerParams(
            collective_id=1, has_side_effects=True, vmem_limit_bytes=VMEM_LIMIT
        ),
    )(part_a, part_b, part_h)


def on_device(owned_blips, potential, slot_owner, slot_row, slot_offset):
    devices = lax.axis_size("dom")
    depth = devices // 8
    rows = owned_blips.shape[0]
    upper = potential if lax.axis_size("grp") == 1 else passed_along(potential, "grp", -1)
    got_a, got_b = gather(owned_blips.reshape(rows, NB, PLANE), depth)
    part_a, part_b, part_h = domain(
        got_a, got_b, potential[0], upper[0], slot_owner.reshape(-1), slot_row, slot_offset, depth
    )
    grad, ham = scatter(part_a, part_b, part_h.reshape(1, devices, 8, -1), depth)
    return grad.reshape(rows, -1), ham


def solution(mesh):
    placed = (
        P(("grp", "dom"), None),
        P("dom", "grp", None),
        P(("grp", "dom"), None),
        P(("grp", "dom")),
        P(("grp", "dom")),
    )
    return jax.shard_map(
        on_device,
        mesh=mesh,
        in_specs=placed,
        out_specs=(P(("grp", "dom"), None), P(("grp", "dom"), None)),
        check_vma=False,
    )
```
